128 devices in a mesh: dp: 4 (over z), expert: 8 (over y, core), tensor: 4 (over x).
Axes of the slice: x: 4, y: 4, z: 4, core: 2. Of those that a mesh axis runs over, the one named last changes fastest.
Arguments:
- layer_in: bfloat16 [2, 512, 4096], P(None, 'dp'), may hold values from -6 to 6
- conv_state: bfloat16 [512, 3, 4096], P('dp', None, ('expert', 'tensor')), may hold values from -6 to 6
- ssm_state: float32 [512, 16, 4096], P('dp', None, ('expert', 'tensor')), may hold values from -6 to 6
- proj_inner: bfloat16 [4096, 4096], P(None, ('expert', 'tensor')), may hold values from -0.09375 to 0.09375
- proj_gate: bfloat16 [4096, 4096], P(None, ('expert', 'tensor')), may hold values from -0.09375 to 0.09375
- conv_weight: float32 [4, 4096], P(None, ('expert', 'tensor')), may hold values from -3 to 3
- conv_bias: float32 [4096], P(('expert', 'tensor')), may hold values from -3 to 3
- delta_down: bfloat16 [4096, 256], P(('expert', 'tensor')), may hold values from -0.09375 to 0.09375
- state_proj: bfloat16 [2, 16, 4096], P(None, None, ('expert', 'tensor')), may hold values from -0.09375 to 0.09375
- delta_up: bfloat16 [256, 4096], P(None, ('expert', 'tensor')), may hold values from -0.375 to 0.375
- delta_bias: float32 [4096], P(('expert', 'tensor')), may hold values from -4 to -1
- decay_log: float32 [16, 4096], P(None, ('expert', 'tensor')), may hold values from 0 to 2.8
- skip_gain: float32 [4096], P(('expert', 'tensor')), may hold values from 0 to 2
- proj_out: bfloat16 [4096, 4096], P(('expert', 'tensor')), may hold values from -0.09375 to 0.09375
- expert_gate: bfloat16 [8, 8192, 4096], P('expert', ('dp', 'tensor')), may hold values from -0.09375 to 0.09375
- expert_up: bfloat16 [8, 8192, 4096], P('expert', ('dp', 'tensor')), may hold values from -0.09375 to 0.09375
- expert_down: bfloat16 [8, 8192, 4096], P('expert', ('dp', 'tensor')), may hold values from -0.0625 to 0.0625
- expert_ids: int32 [2, 512, 2], P(None, ('dp', 'expert', 'tensor')), may hold values from 0 to 7, all different within a row; in each aligned block of 4 rows (0 to 3, 4 to 7, ..., all dimensions but the last counted through in order) at most 2 rows name the same one
- route_weight: float32 [2, 512, 2], P(None, ('dp', 'expert', 'tensor')), may hold values from 0.2 to 1
Outputs:
- layer_out: bfloat16 [2, 512, 4096], P(None, ('dp', 'expert', 'tensor'))
- conv_final: bfloat16 [512, 3, 4096], P('dp', None, ('expert', 'tensor'))
- state_final: float32 [512, 16, 4096], P('dp', None, ('expert', 'tensor'))
The draws below stay inside these ranges and needn't reach their ends.
Inputs may be any that keep to these rules, and one draw needn't show every extreme that they name: `expert_ids`: in each decode step the 4 rows of one device (aligned blocks along the rows) name each expert at most 2 times, and in some devices' rows some expert is named exactly 2 times; the 2 experts of a row differ.
All inputs are finite; a program needn't handle non-finite values.
Results may differ from the reference program's by a relative error of at most 0.023.
Values may be sent and summed in bfloat16 or wider, within the bound.
A program may use at most 128 MiB of HBM per device.

```python
import math
import jax
import jax.numpy as jnp
import numpy as np
from jax import lax

D = 4096
DI = 4096
N = 16
KC = 4
R = 256
EXPERTS = 8
TOP = 2
FF = 8192
STEPS = 2
ROW_DEV = 4
ROWS = 512
CAP = 2
N_DP = 4
N_EXPERT = 8
N_TENSOR = 4


def steps_of(own_key, extent, shards, smallest, high):
    loudness = 1.0
    for axis_at, parts in shards:
        steps = jax.random.uniform(jax.random.fold_in(jax.random.fold_in(own_key, 6), axis_at), (parts,), jnp.float32, smallest / len(shards), high / len(shards))
        loudness = loudness * jnp.repeat(jnp.exp(steps), extent[axis_at] // parts).reshape((-1,) + (1,) * (len(extent) - 1 - axis_at))
    return loudness


def routed_block(stream_key, own, number, rows, count, top, limit, lean):
    sequence = jax.random.permutation(stream_key, count)
    crowded, ordinary = load_shares(count, rows * top, limit, lean, True), load_shares(count, rows * top, limit, lean, False)
    places = jnp.arange(count)

    def named(lengths, offset_by):
        used = int((lengths > 0).sum())
        fixed = max(1, used // 4)
        shifted = fixed + (places - fixed + offset_by * (used - fixed)) % max(1, count - fixed)
        return jnp.zeros((count,), jnp.int32).at[sequence[jnp.where(places < fixed, places, shifted)]].set(jnp.asarray(lengths, jnp.int32))

    lengths = jnp.where(number % 4 == 0, named(crowded, number // 4), named(ordinary, number - number // 4 - 1))
    mixed = jax.random.permutation(jax.random.fold_in(own, 3), count)
    giver, taker = mixed[0:count // 2 * 2:2], mixed[1:count // 2 * 2:2]
    slack = jnp.minimum(lengths[giver] - 1, limit - lengths[taker]) // 2
    slack = jnp.where((giver == sequence[0]) | (taker == sequence[0]) | (lengths[taker] == 0), 0, jnp.maximum(slack, 0))
    shifted = jax.random.randint(jax.random.fold_in(own, 4), (count // 2,), 0, 1 << 20) % (slack + 1)
    lengths = lengths.at[giver].add(-shifted).at[taker].add(shifted)
    items = jnp.searchsorted(jnp.cumsum(lengths), jnp.arange(rows * top), side="right").astype(jnp.int32)
    grid = items.reshape(top, rows).T
    grid = grid[jax.random.permutation(jax.random.fold_in(own, 1), rows)]
    offset_by = jax.random.randint(jax.random.fold_in(own, 2), (rows, 1), 0, top)
    return jnp.take_along_axis(grid, (jnp.arange(top)[None, :] + offset_by) % top, axis=1)


def load_shares(count, total, limit, slope, full):
    weights = [(1 << 20) // math.isqrt(standing ** slope) + 1 for standing in range(1, count + 1)]
    largest = limit if full else min(limit, max(-(-total // count), total * weights[0] // sum(weights)))
    least = 1 if total - largest >= count - 1 else 0
    holding, spare = [largest] + [least] * (count - 1), total - largest - least * (count - 1)
    while spare > 0:
        movable = [i for i in range(1, count) if holding[i] < largest] or [i for i in range(1, count) if holding[i] < limit]
        whole, remaining = sum([weights[i] for i in movable]), spare
        for i in movable:
            extra = min(limit - holding[i], max(1, remaining * weights[i] // whole), spare)
            holding[i] = holding[i] + extra
            spare = spare - extra
    return np.array(holding)


def centred(key, shape, width, reach, pieces=(), kind=jnp.bfloat16):
    factor_of = steps_of(key, shape, pieces, -0.22, 0.18) if pieces else 1.0
    values = jax.random.normal(key, shape, jnp.float32) * width * factor_of
    return jnp.minimum(jnp.maximum(values, -reach), reach).astype(kind)


def setup_inputs(seed: int = 0) -> dict:
    splits = jax.random.split(jax.random.key(seed), 20)
    layer_in = centred(splits[0], (STEPS, ROWS, D), 1.0, 6.0, ((1, 4),))
    conv_state = centred(splits[1], (ROWS, KC - 1, DI), 1.0, 6.0, ((0, 4), (2, 32)))
    ssm_state = centred(splits[2], (ROWS, N, DI), 1.0, 6.0, ((0, 4), (2, 32)), jnp.float32)
    proj_inner = centred(splits[3], (D, DI), D ** -0.5, 0.09375, ((1, 32),))
    proj_gate = centred(splits[4], (D, DI), D ** -0.5, 0.09375, ((1, 32),))
    conv_weight = centred(splits[5], (KC, DI), KC ** -0.5, 3.0, ((1, 32),), jnp.float32)
    conv_bias = centred(splits[6], (DI,), 0.5, 3.0, ((0, 32),), jnp.float32)
    delta_down = centred(splits[7], (DI, R), DI ** -0.5, 0.09375, ((0, 32),))
    state_proj = centred(splits[8], (2, N, DI), DI ** -0.5, 0.09375, ((2, 32),))
    delta_up = centred(splits[9], (R, DI), R ** -0.5, 0.375, ((1, 32),))
    delta_bias = jnp.clip(-4.0 + 3.0 * jax.random.uniform(splits[10], (DI,), jnp.float32) ** steps_of(splits[10], (DI,), ((0, 32),), -0.2, 0.2), -4.0, -1.0)
    decay_log = jnp.clip(2.8 * jax.random.uniform(splits[11], (N, DI), jnp.float32) ** steps_of(splits[11], (N, DI), ((1, 32),), -0.2, 0.2), 0.0, 2.8)
    skip_gain = jnp.clip(2.0 * jax.random.uniform(splits[12], (DI,), jnp.float32) ** steps_of(splits[12], (DI,), ((0, 32),), -0.2, 0.2), 0.0, 2.0)
    proj_out = centred(splits[13], (DI, D), DI ** -0.5, 0.09375, ((0, 32),))
    expert_gate = centred(splits[14], (EXPERTS, FF, D), D ** -0.5, 0.09375, ((0, 8), (1, 16)))
    expert_up = centred(splits[15], (EXPERTS, FF, D), D ** -0.5, 0.09375, ((0, 8), (1, 16)))
    expert_down = centred(splits[16], (EXPERTS, FF, D), FF ** -0.5, 0.0625, ((0, 8), (1, 16)))
    expert_ids_keys = jax.random.split(jax.random.fold_in(splits[17], 1), STEPS * ROWS // ROW_DEV)
    expert_ids_turns = jax.random.permutation(jax.random.fold_in(splits[17], 3), STEPS * ROWS // ROW_DEV)
    expert_ids = jax.vmap(lambda own, number: routed_block(jax.random.fold_in(splits[17], 2), own, number, ROW_DEV, EXPERTS, TOP, CAP, 2))(expert_ids_keys, expert_ids_turns).reshape((STEPS, ROWS, TOP))
    route_weight = jnp.clip(0.2 + 0.8 * jax.random.uniform(splits[18], (STEPS, ROWS, TOP), jnp.float32) ** steps_of(splits[18], (STEPS, ROWS, TOP), ((1, 128),), -0.2, 0.2), 0.2, 1.0)
    return dict(layer_in=layer_in, conv_state=conv_state, ssm_state=ssm_state, proj_inner=proj_inner, proj_gate=proj_gate, conv_weight=conv_weight, conv_bias=conv_bias, delta_down=delta_down, state_proj=state_proj, delta_up=delta_up, delta_bias=delta_bias, decay_log=decay_log, skip_gain=skip_gain, proj_out=proj_out, expert_gate=expert_gate, expert_up=expert_up, expert_down=expert_down, expert_ids=expert_ids, route_weight=route_weight)


def rms_rows(values, eps):
    return values * lax.rsqrt(lax.optimization_barrier(jnp.mean(values * values, axis=-1, keepdims=True)) + eps)

def reference(layer_in, conv_state, ssm_state, proj_inner, proj_gate, conv_weight, conv_bias, delta_down, state_proj, delta_up, delta_bias, decay_log, skip_gain, proj_out, expert_gate, expert_up, expert_down, expert_ids, route_weight):
    slot_limit = N_DP * N_EXPERT * N_TENSOR * CAP
    flat_rows = jnp.arange(ROWS * TOP, dtype=jnp.int32) // TOP
    outputs = []
    for decode in range(STEPS):
        x_float = layer_in[decode].astype(jnp.float32)
        normed = rms_rows(x_float, 1e-06).astype(jnp.bfloat16)
        conv_input = jnp.dot(normed, proj_inner, preferred_element_type=jnp.float32).astype(jnp.bfloat16)
        gate_branch = jnp.dot(normed, proj_gate, preferred_element_type=jnp.float32)
        window = jnp.concatenate([conv_state, conv_input[:, None, :]], axis=1)
        conv_state = window[:, 1:, :]
        conv_sum = conv_bias + lax.optimization_barrier(jnp.sum(window.astype(jnp.float32) * conv_weight[None], axis=1))
        activated = jax.nn.silu(conv_sum).astype(jnp.bfloat16)
        delta_low = jnp.dot(activated, delta_down, preferred_element_type=jnp.float32)
        state_inputs = jnp.einsum('gc,knc->gkn', activated.astype(jnp.float32), state_proj.astype(jnp.float32))
        delta_normed = rms_rows(delta_low, 1e-06).astype(jnp.bfloat16)
        step_size = jax.nn.softplus(jnp.dot(delta_normed, delta_up, preferred_element_type=jnp.float32) + delta_bias)
        act_float = activated.astype(jnp.float32)
        decays = jnp.exp(-step_size[:, None, :] * jnp.exp(decay_log)[None])
        ssm_state = decays * ssm_state + step_size[:, None, :] * state_inputs[:, 0, :, None] * act_float[:, None, :]
        readout = lax.optimization_barrier(jnp.sum(ssm_state * state_inputs[:, 1, :, None], axis=1))
        gated_out = ((readout + skip_gain * act_float) * jax.nn.silu(gate_branch)).astype(jnp.bfloat16)
        residual = x_float + jnp.dot(gated_out, proj_out, preferred_element_type=jnp.float32)
        expert_in = rms_rows(residual, 1e-06).astype(jnp.bfloat16)
        flat_ids = expert_ids[decode].reshape(-1).astype(jnp.int32)
        flat_weight = route_weight[decode].reshape(-1)

        def one_expert(expert):
            mismatch = (flat_ids != expert).astype(jnp.int32)
            sorted_at = jnp.argsort(mismatch, stable=True)[:slot_limit]
            live_mask = (mismatch[sorted_at] == 0).astype(jnp.float32)
            row_index = flat_rows[sorted_at]
            selected = expert_in[row_index]
            gate_proj = jnp.dot(selected, expert_gate[expert].T, preferred_element_type=jnp.float32)
            up_proj = jnp.dot(selected, expert_up[expert].T, preferred_element_type=jnp.float32)
            activation = (jax.nn.silu(gate_proj) * up_proj).astype(jnp.bfloat16)
            expert_out = jnp.dot(activation, expert_down[expert], preferred_element_type=jnp.float32).astype(jnp.bfloat16)
            expert_out = lax.optimization_barrier(expert_out).astype(jnp.float32)
            return (expert_out * (flat_weight[sorted_at] * live_mask)[:, None], row_index)
        contribs, row_lists = lax.map(one_expert, jnp.arange(EXPERTS, dtype=jnp.int32))
        expert_sum = jnp.zeros((ROWS, D), jnp.float32).at[row_lists.reshape(-1)].add(contribs.reshape(-1, D))
        outputs.append((residual + expert_sum).astype(jnp.bfloat16))
    return (jnp.stack(outputs), conv_state, ssm_state)
```

```python
import functools

import jax
import jax.numpy as jnp
from jax import lax
from jax.experimental import pallas as pl
from jax.experimental.pallas import tpu as pltpu
from jax.sharding import PartitionSpec as P

MESH = pl.DeviceIdType.MESH
F32 = jnp.float32
BF16 = jnp.bfloat16
MIB = 2**20


def place():
    z, e, x = lax.axis_index("dp"), lax.axis_index("expert"), lax.axis_index("tensor")
    return z, lax.div(e, 2), lax.rem(e, 2), x


def remote(src, dst, sems, at, device):
    return pltpu.make_async_remote_copy(
        src_ref=src,
        dst_ref=dst,
        send_sem=sems[0].at[at],
        recv_sem=sems[1].at[at],
        device_id=device,
        device_id_type=MESH,
    )


def greet(devices):
    barrier = pltpu.get_barrier_semaphore()
    for device in devices:
        pl.semaphore_signal(barrier, inc=1, device_id=device, device_id_type=MESH)
    pl.semaphore_wait(barrier, len(devices))


def small_sum_kernel(part, out, recv, send_a, recv_a, send_b, recv_b):
    z, y, c, x = place()
    me = (y * 2 + c) * 4 + x

    def device(p):
        return (z, lax.div(p, 4), lax.rem(p, 4))

    barrier = pltpu.get_barrier_semaphore()

    def signal(i, carry):
        pl.semaphore_signal(
            barrier, inc=1, device_id=device(lax.rem(me + i, 32)), device_id_type=MESH
        )
        return carry

    lax.fori_loop(1, 32, signal, 0)
    pl.semaphore_wait(barrier, 31)

    def first(i):
        p = lax.rem(me + i, 32)
        return remote(part.at[p], recv.at[i - 1], (send_a, recv_a), i - 1, device(p))

    def start_first(i, carry):
        first(i).start()
        return carry

    lax.fori_loop(1, 32, start_first, 0)

    def add(i, total):
        first(i).wait()
        return total + recv[i - 1].astype(F32)

    total = lax.fori_loop(1, 32, add, part[me].astype(F32))
    low, state = total[:8], total[8:]
    normed = low * lax.rsqrt(jnp.mean(low * low, axis=-1, keepdims=True) + 1e-06)
    high = state.astype(BF16)
    rest = state - high.astype(F32)
    shifted = jnp.concatenate([high.astype(F32)[:, :32], rest[:, :32], state[:, 64:]], axis=1)
    out[me] = jnp.concatenate([normed, shifted], axis=0).astype(BF16)

    def second(i):
        p = lax.rem(me + i, 32)
        return remote(out.at[me], out.at[me], (send_b, recv_b), i - 1, device(p))

    def second_from(i):
        p = lax.rem(me + 32 - i, 32)
        return remote(out.at[p], out.at[p], (send_b, recv_b), i - 1, device(p))

    def start_second(i, carry):
        second(i).start()
        return carry

    lax.fori_loop(1, 32, start_second, 0)

    def wait_second(i, carry):
        second(i).wait_send()
        second_from(i).wait_recv()
        return carry

    lax.fori_loop(1, 32, wait_second, 0)


def small_sum(part):
    return pl.pallas_call(
        small_sum_kernel,
        out_shape=jax.ShapeDtypeStruct((32, 16, 256), BF16),
        in_specs=[pl.BlockSpec(memory_space=pltpu.VMEM)],
        out_specs=pl.BlockSpec(memory_space=pltpu.VMEM),
        scratch_shapes=[
            pltpu.VMEM((31, 16, 256), BF16),
            pltpu.SemaphoreType.DMA((31,)),
            pltpu.SemaphoreType.DMA((31,)),
            pltpu.SemaphoreType.DMA((31,)),
            pltpu.SemaphoreType.DMA((31,)),
        ],
        compiler_params=pltpu.CompilerParams(
            collective_id=0, has_side_effects=True, vmem_limit_bytes=16 * MIB
        ),
        name="small_sum",
    )(part)


def mixer_out_kernel(
    gated, weight, own, res, first, mine, got0, sum_a, sum_b, got1, mid, got2, last, got3, ss, rs
):
    z, y, c, x = place()
    sems = (ss, rs)

    def dev(dy=0, dc=0, dx=0):
        return (z, lax.rem(y + dy, 4) * 2 + lax.rem(c + dc, 2), lax.rem(x + dx, 4))

    greet([dev(dc=1)] + [dev(dx=d) for d in (1, 2, 3)] + [dev(dy=d) for d in (1, 2, 3)])
    other = 1 - c
    left = gated[...]
    swaps = []
    for q in range(2):
        cols = pl.ds(pl.multiple_of(other * 2048 + q * 1024, 1024), 1024)
        first[q] = jnp.dot(left, weight[:, cols], preferred_element_type=F32).astype(BF16)
        swap = remote(first.at[q], got0.at[q], sems, q, dev(dc=1))
        swap.start()
        swaps.append(swap)
    for q in range(2):
        cols = pl.ds(pl.multiple_of(c * 2048 + q * 1024, 1024), 1024)
        mine[q] = jnp.dot(left, weight[:, cols], preferred_element_type=F32)
    ones = []
    for q in range(2):
        swaps[q].wait()
        both = mine[q] + got0[q].astype(F32)
        mine[q] = both
        blocks = both.astype(BF16).reshape(4, 4, 16, 1024)
        if q == 0:
            for at in range(4):
                for to in range(4):
                    sum_a[to, at] = blocks[at, to]
        else:
            sum_b[...] = blocks
        for d in (1, 2, 3):
            if q == 0:
                copy = remote(
                    sum_a.at[lax.rem(x + d, 4)], got1.at[0, d - 1], sems, 2 + d - 1, dev(dx=d)
                )
            else:
                copy = remote(
                    sum_b.at[lax.rem(y + d, 4)], got1.at[1, d - 1], sems, 5 + d - 1, dev(dy=d)
                )
            copy.start()
            ones.append(copy)
    twos = []
    for q in range(2):
        for d in range(3):
            ones[q * 3 + d].wait()
        kept = sum_a[x] if q == 0 else sum_b[y]
        total = kept.astype(F32)
        for d in range(3):
            total = total + got1[q, d].astype(F32)
        mid[q] = total.astype(BF16)
        for d in (1, 2, 3):
            if q == 0:
                copy = remote(
                    mid.at[0, lax.rem(y + d, 4)], got2.at[0, d - 1], sems, 8 + d - 1, dev(dy=d)
                )
            else:
                copy = remote(
                    mid.at[1, lax.rem(x + d, 4)], got2.at[1, d - 1], sems, 11 + d - 1, dev(dx=d)
                )
            copy.start()
            twos.append(copy)
    for q in range(2):
        for d in range(3):
            twos[q * 3 + d].wait()
        total = (mid[0, y] if q == 0 else mid[1, x]).astype(F32)
        for d in range(3):
            total = total + got2[q, d].astype(F32)
        last[:, :, q * 1024 : (q + 1) * 1024] = total.reshape(2, 8, 1024)
    swap = remote(last.at[other], got3, sems, 14, dev(dc=1))
    swap.start()
    here = pl.ds(pl.multiple_of(c * 2048, 2048), 2048)
    there = pl.ds(pl.multiple_of(other * 2048, 2048), 2048)
    res[:, here] = last[c] + own[:, here].astype(F32)
    swap.wait()
    res[:, there] = got3[...] + own[:, there].astype(F32)


def mixer_out(gated, weight, own):
    return pl.pallas_call(
        mixer_out_kernel,
        out_shape=jax.ShapeDtypeStruct((8, 4096), F32),
        in_specs=[pl.BlockSpec(memory_space=pltpu.VMEM)] * 3,
        out_specs=pl.BlockSpec(memory_space=pltpu.VMEM),
        scratch_shapes=[
            pltpu.VMEM((2, 256, 1024), BF16),
            pltpu.VMEM((2, 256, 1024), F32),
            pltpu.VMEM((2, 256, 1024), BF16),
            pltpu.VMEM((4, 4, 16, 1024), BF16),
            pltpu.VMEM((4, 4, 16, 1024), BF16),
            pltpu.VMEM((2, 3, 4, 16, 1024), BF16),
            pltpu.VMEM((2, 4, 16, 1024), BF16),
            pltpu.VMEM((2, 3, 16, 1024), BF16),
            pltpu.VMEM((2, 8, 2048), F32),
            pltpu.VMEM((8, 2048), F32),
            pltpu.SemaphoreType.DMA((15,)),
            pltpu.SemaphoreType.DMA((15,)),
        ],
        compiler_params=pltpu.CompilerParams(
            collective_id=1, has_side_effects=True, vmem_limit_bytes=24 * MIB
        ),
        name="mixer_out",
    )(gated, weight, own)


GATHER = 14


def expert_kernel(
    res, spread, gather_perm, back_perm, mix_high, mix_low, gate_hbm, up_hbm, down_hbm,
    out,
    gate, up, down, message, arrived, rows, act, part, hop, hop2, got_hop, got_full, quad, got_quad,
    reply, returned, local, ss, rs,
):
    z, y, c, x = place()
    e = y * 2 + c
    sems = (ss, rs)
    loads = []
    for i, (a, b) in enumerate(((gate_hbm, gate), (up_hbm, up), (down_hbm, down))):
        load = pltpu.make_async_copy(a.at[0], b, local.at[i])
        load.start()
        loads.append(load)

    def dev_e(d):
        return (z, lax.rem(e + d, 8), x)

    def dev_x(d):
        return (z, e, lax.rem(x + d, 4))

    def dev_z(d):
        return (lax.rem(z + d, 4), e, x)

    residual = res[...]
    normed = residual * lax.rsqrt(jnp.mean(residual * residual, axis=-1, keepdims=True) + 1e-06)
    stacked = jnp.concatenate([normed[:, k * 512 : (k + 1) * 512] for k in range(8)], axis=0)
    spread_rows = jnp.dot(spread[...], stacked.astype(BF16), preferred_element_type=F32)
    message[...] = spread_rows.astype(BF16).reshape(2, 8, 16, 512)
    greet([dev_e(d) for d in range(1, 8)] + [f(d) for f in (dev_x, dev_z) for d in (1, 2, 3)])

    sends = {}
    for s in range(2):
        for d in range(1, 8):
            copy = remote(
                message.at[s, lax.rem(e + d, 8)],
                arrived.at[s, e],
                sems,
                s * 7 + d - 1,
                dev_e(d),
            )
            copy.start()
            sends[s, d] = copy
        arrived[s, e] = message[s, e]

    base = 14
    halves = (pl.ds(0, 2048), pl.ds(2048, 2048))

    def first_gather(s):
        for d in range(1, 8):
            sends[s, d].wait()
        ordered = jnp.dot(
            gather_perm[...], arrived[s].reshape(128, 512), preferred_element_type=F32
        ).astype(BF16)
        for k in range(8):
            h, at = divmod(k, 4)
            rows[s, h, z, x, :, at * 512 : (at + 1) * 512] = ordered[k * 16 : (k + 1) * 16]
        copies = []
        for h in range(2):
            for d in (1, 2, 3):
                copy = remote(
                    rows.at[s, h, z, x],
                    rows.at[s, h, z, x],
                    sems,
                    base + s * GATHER + h * 3 + d - 1,
                    (dev_x if h == 0 else dev_z)(d),
                )
                copy.start()
                copies.append(copy)
        return copies

    def band(s, h, at, half=None):
        along = pl.ds(0, 4) if half is None else pl.ds(2 * half, 2)
        return rows.at[s, h, at, along] if h == 0 else rows.at[s, h, along, at]

    def second_gather(s, firsts):
        copies = []
        at0 = base + s * GATHER + 6
        for h in range(2):
            for copy in firsts[h * 3 : h * 3 + 3]:
                copy.wait()
            dev, at = (dev_z, z) if h == 0 else (dev_x, x)
            for i, d in enumerate((1, 3)):
                copy = remote(band(s, h, at), band(s, h, at), sems, at0 + h * 4 + i, dev(d))
                copy.start()
                copies.append(copy)
        return copies

    def third_gather(s, seconds):
        copies = []
        at0 = base + s * GATHER + 6
        for h in range(2):
            dev, at = (dev_z, z) if h == 0 else (dev_x, x)
            for i, d in enumerate((1, 3)):
                seconds[h * 2 + i].wait()
                source = lax.rem(at + 4 - d, 4)
                copy = remote(
                    band(s, h, source, i), band(s, h, source, i), sems, at0 + h * 4 + 2 + i, dev(d)
                )
                copy.start()
                copies.append(copy)
        return copies

    def compute(s):
        wide = 256

        def hidden(t, carry):
            at = pl.ds(pl.multiple_of(t * wide, wide), wide)
            g = jnp.zeros((256, wide), F32)
            u = jnp.zeros((256, wide), F32)
            for h in range(2):
                piece = rows[s, h].reshape(256, 2048)
                nt = (((1,), (1,)), ((), ()))
                g = g + lax.dot_general(piece, gate[at, halves[h]], nt, preferred_element_type=F32)
                u = u + lax.dot_general(piece, up[at, halves[h]], nt, preferred_element_type=F32)
            act[:, at] = (g / (1.0 + jnp.exp(-g)) * u).astype(BF16)
            return carry

        lax.fori_loop(0, 512 // wide, hidden, 0)

    def project(s):
        for h in range(2):

            def columns(t, carry, h=h):
                at = pl.ds(pl.multiple_of(t * 512, 512), 512)
                from_ = pl.ds(pl.multiple_of(h * 2048 + t * 512, 512), 512)
                value = jnp.dot(act[...], down[:, from_], preferred_element_type=F32)
                part[s, h, :, :, :, at] = value.astype(BF16).reshape(4, 4, 16, 512)
                return carry

            lax.fori_loop(0, 4, columns, 0)

    base2 = base + 2 * GATHER

    def pband(ref, h, at, half=None):
        along = pl.ds(0, 4) if half is None else pl.ds(2 * half, 2)
        return ref.at[h, at, along] if h == 0 else ref.at[h, along, at]

    def first_reduce(s):
        copies = []
        for h in range(2):
            dev, at = (dev_z, z) if h == 0 else (dev_x, x)
            far = lax.rem(at + 2, 4)
            for i, d in enumerate((1, 3)):
                copy = remote(
                    pband(part.at[s], h, far, i),
                    got_hop.at[s, h, i],
                    sems,
                    base2 + s * GATHER + h * 4 + i,
                    dev(d),
                )
                copy.start()
                copies.append(copy)
        return copies

    def second_reduce(s, firsts):
        copies = []
        for h in range(2):
            dev, at = (dev_z, z) if h == 0 else (dev_x, x)
            for i, d in enumerate((1, 3)):
                firsts[h * 2 + i].wait()
                to = lax.rem(at + d, 4)
                if h == 0:
                    value = part[s, h, to, 2 * i : 2 * i + 2].astype(F32)
                    part[s, h, to, 2 * i : 2 * i + 2] = (
                        value + got_hop[s, h, i].astype(F32)
                    ).astype(BF16)
                else:
                    for j in range(2):
                        value = part[s, h, 2 * i + j, to].astype(F32)
                        part[s, h, 2 * i + j, to] = (
                            value + got_hop[s, h, i, j].astype(F32)
                        ).astype(BF16)
                copy = remote(
                    pband(part.at[s], h, to),
                    got_full.at[s, h, i],
                    sems,
                    base2 + s * GATHER + h * 4 + 2 + i,
                    dev(d),
                )
                copy.start()
                copies.append(copy)
        return copies

    def third_reduce(s, seconds):
        copies = []
        for h in range(2):
            for i in range(2):
                seconds[h * 2 + i].wait()
            for j in range(4):
                kept = part[s, h, z, j] if h == 0 else part[s, h, j, x]
                total = kept.astype(F32)
                for i in range(2):
                    total = total + got_full[s, h, i, j].astype(F32)
                quad[s, h, j] = total.astype(BF16)
            dev, at = (dev_x, x) if h == 0 else (dev_z, z)
            for d in (1, 2, 3):
                copy = remote(
                    quad.at[s, h, lax.rem(at + d, 4)],
                    got_quad.at[s, h, d - 1],
                    sems,
                    base2 + s * GATHER + 8 + h * 3 + d - 1,
                    dev(d),
                )
                copy.start()
                copies.append(copy)
        return copies

    base3 = base2 + 2 * GATHER

    def send_back(s, thirds):
        pieces = []
        for h in range(2):
            for copy in thirds[h * 3 : h * 3 + 3]:
                copy.wait()
            at = x if h == 0 else z
            total = quad[s, h, at].astype(F32)
            for d in range(3):
                total = total + got_quad[s, h, d].astype(F32)
            total = total.astype(BF16)
            pieces.extend(total[:, k * 512 : (k + 1) * 512] for k in range(4))
        stack = jnp.concatenate(pieces, axis=0)
        value = jnp.dot(back_perm[...], stack, preferred_element_type=F32).astype(BF16)
        reply[s] = value.reshape(8, 16, 512)
        copies = []
        for d in range(1, 8):
            copy = remote(
                reply.at[s, lax.rem(e + d, 8)],
                returned.at[s, e],
                sems,
                base3 + s * 7 + d - 1,
                dev_e(d),
            )
            copy.start()
            copies.append(copy)
        returned[s, e] = reply[s, e]
        return copies

    first0 = first_gather(0)
    first1 = first_gather(1)
    second0 = second_gather(0, first0)
    third0 = third_gather(0, second0)
    second1 = second_gather(1, first1)
    for copy in third0:
        copy.wait()
    for load in loads[:2]:
        load.wait()
    compute(0)
    third1 = third_gather(1, second1)
    loads[2].wait()
    project(0)
    hop0 = first_reduce(0)
    for copy in third1:
        copy.wait()
    full0 = second_reduce(0, hop0)
    compute(1)
    project(1)
    hop1 = first_reduce(1)
    quad0 = third_reduce(0, full0)
    full1 = second_reduce(1, hop1)
    back0 = send_back(0, quad0)
    quad1 = third_reduce(1, full1)
    back1 = send_back(1, quad1)
    for copy in back0 + back1:
        copy.wait()
    replies = returned[...].reshape(256, 512)
    value = jnp.dot(mix_high[...], replies, preferred_element_type=F32)
    value = value + jnp.dot(mix_low[...], replies, preferred_element_type=F32)
    for k in range(8):
        cols = slice(k * 512, (k + 1) * 512)
        out[:, cols] = res[:, cols] + value[k * 8 : (k + 1) * 8]


def expert_layer(res, spread, gather_perm, back_perm, mix_high, mix_low, gate, up, down):
    vmem = pl.BlockSpec(memory_space=pltpu.VMEM)
    hbm = pl.BlockSpec(memory_space=pl.ANY)
    count = 14 + 4 * GATHER + 14
    return pl.pallas_call(
        expert_kernel,
        out_shape=jax.ShapeDtypeStruct((8, 4096), F32),
        in_specs=[vmem] * 6 + [hbm] * 3,
        out_specs=vmem,
        scratch_shapes=[
            pltpu.VMEM((512, 4096), BF16),
            pltpu.VMEM((512, 4096), BF16),
            pltpu.VMEM((512, 4096), BF16),
            pltpu.VMEM((2, 8, 16, 512), BF16),
            pltpu.VMEM((2, 8, 16, 512), BF16),
            pltpu.VMEM((2, 2, 4, 4, 16, 2048), BF16),
            pltpu.VMEM((256, 512), BF16),
            pltpu.VMEM((2, 2, 4, 4, 16, 2048), BF16),
            pltpu.VMEM((16, 128), BF16),
            pltpu.VMEM((16, 128), BF16),
            pltpu.VMEM((2, 2, 2, 2, 16, 2048), BF16),
            pltpu.VMEM((2, 2, 2, 4, 16, 2048), BF16),
            pltpu.VMEM((2, 2, 4, 16, 2048), BF16),
            pltpu.VMEM((2, 2, 3, 16, 2048), BF16),
            pltpu.VMEM((2, 8, 16, 512), BF16),
            pltpu.VMEM((2, 8, 16, 512), BF16),
            pltpu.SemaphoreType.DMA((3,)),
            pltpu.SemaphoreType.DMA((count,)),
            pltpu.SemaphoreType.DMA((count,)),
        ],
        compiler_params=pltpu.CompilerParams(
            collective_id=2, has_side_effects=True, vmem_limit_bytes=48 * MIB
        ),
        name="experts",
    )(res, spread, gather_perm, back_perm, mix_high, mix_low, gate, up, down)


def tables(expert_ids, route_weight):
    named = expert_ids[..., None] == jnp.arange(8, dtype=jnp.int32)
    hit = jnp.any(named, axis=2)
    earlier = jnp.arange(4)[:, None] > jnp.arange(4)[None, :]
    slot = jnp.sum((earlier[None, :, :, None] & hit[:, None, :, :]).astype(jnp.int32), axis=2)
    chosen = hit[..., None] & (slot[..., None] == jnp.arange(2))
    weight = jnp.sum(jnp.where(named, route_weight[..., None], 0.0), axis=2)
    same_step = jnp.eye(2, dtype=bool)
    same_chunk = jnp.eye(8, dtype=bool)
    pick = jnp.transpose(chosen, (0, 2, 3, 1))[:, :, None, :, None, None, :]
    mask = (
        pick
        & same_chunk[None, None, :, None, :, None, None]
        & same_step[:, None, None, None, None, :, None]
    )
    weights = jnp.transpose(weight, (0, 2, 1))[:, :, None, None, None, None, :]
    spread = mask.astype(BF16).reshape(256, 64)
    mix = jnp.where(mask, weights, 0.0).reshape(256, 64).T
    high = mix.astype(BF16)
    low = (mix - high.astype(F32)).astype(BF16)
    return spread, high, low


def shards(
    layer_in,
    conv_state,
    ssm_state,
    proj_inner,
    proj_gate,
    conv_weight,
    conv_bias,
    delta_down,
    state_proj,
    delta_up,
    delta_bias,
    decay_log,
    skip_gain,
    proj_out,
    expert_gate,
    expert_up,
    expert_down,
    expert_ids,
    route_weight,
):
    spread, mix_high, mix_low = tables(expert_ids, route_weight)
    index = jnp.arange(128)
    chunk, source, slot = index // 16, index // 2 % 8, index % 2
    gather_perm = ((source * 16 + chunk * 2 + slot)[:, None] == index[None, :]).astype(BF16)
    back_perm = gather_perm.T

    flat = layer_in.reshape(256, 4096)
    flat_float = flat.astype(F32)
    scale = lax.rsqrt(jnp.mean(flat_float * flat_float, axis=-1, keepdims=True) + 1e-06)
    conv_in = (jnp.dot(flat, proj_inner, preferred_element_type=F32) * scale).astype(BF16)
    gate_branch = jnp.dot(flat, proj_gate, preferred_element_type=F32) * scale
    steps = [conv_state[:, 0], conv_state[:, 1], conv_state[:, 2], conv_in[:128], conv_in[128:]]
    floats = [v.astype(F32) for v in steps]
    acts = []
    for s in range(2):
        total = conv_bias[None]
        for k in range(4):
            total = total + floats[s + k] * conv_weight[k][None]
        acts.append(jax.nn.silu(total).astype(BF16))
    activated = jnp.concatenate(acts, axis=0)
    conv_final = jnp.stack(steps[2:], axis=1)
    delta_part = jnp.dot(activated, delta_down, preferred_element_type=F32).astype(BF16)
    state_part = lax.dot_general(
        activated,
        state_proj.reshape(32, 128),
        (((1,), (1,)), ((), ())),
        preferred_element_type=F32,
    ).astype(BF16)
    state_part = jnp.pad(state_part, ((0, 0), (0, 224)))
    both = jnp.stack([delta_part, state_part], axis=0).reshape(2, 2, 32, 4, 256)
    part = jnp.transpose(both, (2, 0, 1, 3, 4)).reshape(32, 16, 256)
    summed = small_sum(part).reshape(32, 2, 2, 4, 256)
    delta_normed = jnp.transpose(summed[:, 0], (1, 0, 2, 3)).reshape(256, 256)
    state_in = jnp.transpose(summed[:, 1, :, :, :64], (1, 0, 2, 3)).reshape(2, 128, 64)
    state_in = state_in[..., :32].astype(F32) + state_in[..., 32:].astype(F32)
    step_size = jax.nn.softplus(
        jnp.dot(delta_normed, delta_up, preferred_element_type=F32) + delta_bias
    ).reshape(2, 128, 128)
    rates = jnp.exp(decay_log)[None]
    act_float = activated.astype(F32).reshape(2, 128, 128)
    gate_branch = gate_branch.reshape(2, 128, 128)
    gated = []
    for s in range(2):
        size = step_size[s][:, None, :]
        ssm_state = (
            jnp.exp(-size * rates) * ssm_state
            + size * state_in[s, :, :16, None] * act_float[s][:, None, :]
        )
        readout = jnp.sum(ssm_state * state_in[s, :, 16:, None], axis=1)
        gated.append(
            ((readout + skip_gain * act_float[s]) * jax.nn.silu(gate_branch[s])).astype(BF16)
        )
    gated = jnp.stack(gated).reshape(2, 4, 2, 4, 4, 128)
    gated = jnp.transpose(gated, (1, 3, 2, 0, 4, 5)).reshape(256, 128)
    place_ = lax.axis_index(("expert", "tensor"))
    own = lax.dynamic_slice_in_dim(layer_in, place_ * 4, 4, 1).reshape(8, 4096)
    residual = mixer_out(gated, proj_out, own)
    out = expert_layer(
        residual, spread, gather_perm, back_perm, mix_high, mix_low,
        expert_gate, expert_up, expert_down,
    )
    layer_out = out.astype(BF16).reshape(2, 4, 4096)
    return (layer_out, conv_final, ssm_state)


def solution(mesh):
    channels = ("expert", "tensor")
    rows = ("dp", "expert", "tensor")
    placed = (
        P(None, "dp", None),
        P("dp", None, channels),
        P("dp", None, channels),
        P(None, channels),
        P(None, channels),
        P(None, channels),
        P(channels),
        P(channels, None),
        P(None, None, channels),
        P(None, channels),
        P(channels),
        P(None, channels),
        P(channels),
        P(channels, None),
        P("expert", ("dp", "tensor"), None),
        P("expert", ("dp", "tensor"), None),
        P("expert", ("dp", "tensor"), None),
        P(None, rows, None),
        P(None, rows, None),
    )
    return jax.shard_map(
        shards,
        mesh=mesh,
        in_specs=placed,
        out_specs=(P(None, rows, None), P("dp", None, channels), P("dp", None, channels)),
        check_vma=False,
    )
```

```python
import functools

import jax
import jax.numpy as jnp
from jax import lax
from jax.experimental import pallas as pl
from jax.experimental.pallas import tpu as pltpu
from jax.sharding import PartitionSpec as P

MESH = pl.DeviceIdType.MESH
F32 = jnp.float32
BF16 = jnp.bfloat16
MIB = 2**20


def place():
    z, e, x = lax.axis_index("dp"), lax.axis_index("expert"), lax.axis_index("tensor")
    return z, lax.div(e, 2), lax.rem(e, 2), x


def remote(src, dst, sems, at, device):
    return pltpu.make_async_remote_copy(
        src_ref=src,
        dst_ref=dst,
        send_sem=sems[0].at[at],
        recv_sem=sems[1].at[at],
        device_id=device,
        device_id_type=MESH,
    )


def greet(devices):
    barrier = pltpu.get_barrier_semaphore()
    for device in devices:
        pl.semaphore_signal(barrier, inc=1, device_id=device, device_id_type=MESH)
    pl.semaphore_wait(barrier, len(devices))


def silu(v):
    return v / (1.0 + jnp.exp(-v))


PIECES = 4


def mixer_in_kernel(
    rows_hbm, inner_hbm, gate_hbm, conv_state, conv_weight, conv_bias, delta_down, state_proj,
    delta_up, delta_bias,
    conv_out, act_out, gate_out, size_out, state_out,
    rows, inner, gate, local, part, got, both, recv, out, one, other, send_a, recv_a, send_b, recv_b,
):
    z, y, c, x = place()
    me = y * 4 + x
    width = 4096 // PIECES
    loads = []
    for k in range(PIECES):
        cut = pl.ds(k * width, width)
        three = []
        for i, (a, b) in enumerate(
            (
                (rows_hbm.at[:, cut], rows.at[:, cut]),
                (inner_hbm.at[cut], inner.at[cut]),
                (gate_hbm.at[cut], gate.at[cut]),
            )
        ):
            load = pltpu.make_async_copy(a, b, local.at[k * 3 + i])
            load.start()
            three.append(load)
        loads.append(three)

    def chip(p):
        return (z, lax.div(p, 4) * 2 + c, lax.rem(p, 4))

    sibling = (z, y * 2 + 1 - c, x)
    barrier = pltpu.get_barrier_semaphore()
    pl.semaphore_signal(barrier, inc=1, device_id=sibling, device_id_type=MESH)

    def signal(i, carry):
        pl.semaphore_signal(
            barrier, inc=1, device_id=chip(lax.rem(me + i, 16)), device_id_type=MESH
        )
        return carry

    lax.fori_loop(1, 16, signal, 0)

    squares = jnp.zeros((256, 1), F32)
    conv_in = jnp.zeros((256, 128), F32)
    for k in range(PIECES):
        loads[k][0].wait()
        loads[k][1].wait()
        piece = rows[:, k * width : (k + 1) * width]
        conv_in = conv_in + jnp.dot(
            piece, inner[k * width : (k + 1) * width], preferred_element_type=F32
        )
        wide = piece.astype(F32)
        squares = squares + jnp.sum(wide * wide, axis=1, keepdims=True)
    scale = lax.rsqrt(squares * (1.0 / 4096) + 1e-06)
    conv_in = (conv_in * scale).astype(BF16)
    conv_out[...] = conv_in
    conv_in = conv_in.astype(F32)
    window = [conv_state[k].astype(F32) for k in range(3)] + [conv_in[:128], conv_in[128:]]
    acts = []
    for s in range(2):
        total = conv_bias[...]
        for k in range(4):
            total = total + window[s + k] * conv_weight[k : k + 1]
        acts.append(silu(total))
    activated = jnp.concatenate(acts, axis=0).astype(BF16)
    act_out[...] = activated
    delta = jnp.dot(activated, delta_down[...], preferred_element_type=F32)
    state = lax.dot_general(
        activated, state_proj[...], (((1,), (1,)), ((), ())), preferred_element_type=F32
    )
    state = jnp.concatenate([state, jnp.zeros((256, 224), F32)], axis=1)
    blocks = jnp.concatenate([delta.reshape(32, 8, 256), state.reshape(32, 8, 256)], axis=1)
    part[...] = blocks.astype(BF16).reshape(2, 16, 16, 256)

    pl.semaphore_wait(barrier, 16)
    swap = remote(part.at[1 - c], got, (one, other), 0, sibling)
    swap.start()
    swap.wait()
    both[...] = (part[c].astype(F32) + got[...].astype(F32)).astype(BF16)

    def first(i):
        p = lax.rem(me + i, 16)
        return remote(both.at[p], recv.at[i - 1], (send_a, recv_a), i - 1, chip(p))

    def start_first(i, carry):
        first(i).start()
        return carry

    lax.fori_loop(1, 16, start_first, 0)

    gated = jnp.zeros((256, 128), F32)
    for k in range(PIECES):
        loads[k][2].wait()
        gated = gated + jnp.dot(
            rows[:, k * width : (k + 1) * width],
            gate[k * width : (k + 1) * width],
            preferred_element_type=F32,
        )
    gate_out[...] = silu(gated * scale)

    def add(i, total):
        first(i).wait()
        return total + recv[i - 1].astype(F32)

    total = lax.fori_loop(1, 16, add, both[me].astype(F32))
    low, state = total[:8], total[8:]
    normed = low * lax.rsqrt(jnp.mean(low * low, axis=-1, keepdims=True) + 1e-06)
    high = state.astype(BF16).astype(F32)
    rest = state - high
    split = jnp.concatenate([high[:, :32], rest[:, :32], state[:, 64:]], axis=1)
    out[c, me] = jnp.concatenate([normed, split], axis=0).astype(BF16)

    def second(i):
        return remote(
            out.at[c, me], out.at[c, me], (send_b, recv_b), i - 1, chip(lax.rem(me + i, 16))
        )

    def second_from(i):
        p = lax.rem(me + 16 - i, 16)
        return remote(out.at[c, p], out.at[c, p], (send_b, recv_b), i - 1, chip(p))

    def start_second(i, carry):
        second(i).start()
        return carry

    lax.fori_loop(1, 16, start_second, 0)

    def wait_second(i, carry):
        second(i).wait_send()
        second_from(i).wait_recv()
        return carry

    lax.fori_loop(1, 16, wait_second, 0)
    swap = remote(out.at[c], out.at[c], (one, other), 1, sibling)
    swap.start()
    swap.wait_send()
    remote(out.at[1 - c], out.at[1 - c], (one, other), 1, sibling).wait_recv()
    summed = out[...].reshape(32, 16, 256).astype(F32)
    normed = summed[:, :8].reshape(256, 256).astype(BF16)
    value = jnp.dot(normed, delta_up[...], preferred_element_type=F32) + delta_bias[...]
    size_out[...] = jnp.maximum(value, 0.0) + jnp.log1p(jnp.exp(-jnp.abs(value)))
    state = summed[:, 8:].reshape(256, 256)
    state_out[...] = state[:, :32] + state[:, 32:64]


def mixer_in(rows, inner, gate, *rest):
    vmem = pl.BlockSpec(memory_space=pltpu.VMEM)
    hbm = pl.BlockSpec(memory_space=pl.ANY)
    return pl.pallas_call(
        mixer_in_kernel,
        out_shape=(
            jax.ShapeDtypeStruct((256, 128), BF16),
            jax.ShapeDtypeStruct((256, 128), BF16),
            jax.ShapeDtypeStruct((256, 128), F32),
            jax.ShapeDtypeStruct((256, 128), F32),
            jax.ShapeDtypeStruct((256, 32), F32),
        ),
        in_specs=[hbm] * 3 + [vmem] * len(rest),
        out_specs=(vmem,) * 5,
        scratch_shapes=[
            pltpu.VMEM((256, 4096), BF16),
            pltpu.VMEM((4096, 128), BF16),
            pltpu.VMEM((4096, 128), BF16),
            pltpu.SemaphoreType.DMA((3 * PIECES,)),
            pltpu.VMEM((2, 16, 16, 256), BF16),
            pltpu.VMEM((16, 16, 256), BF16),
            pltpu.VMEM((16, 16, 256), BF16),
            pltpu.VMEM((15, 16, 256), BF16),
            pltpu.VMEM((2, 16, 16, 256), BF16),
            pltpu.SemaphoreType.DMA((2,)),
            pltpu.SemaphoreType.DMA((2,)),
            pltpu.SemaphoreType.DMA((15,)),
            pltpu.SemaphoreType.DMA((15,)),
            pltpu.SemaphoreType.DMA((15,)),
            pltpu.SemaphoreType.DMA((15,)),
        ],
        compiler_params=pltpu.CompilerParams(
            collective_id=0, has_side_effects=True, vmem_limit_bytes=56 * MIB
        ),
        name="mixer_in",
    )(rows, inner, gate, *rest)


def tables(ids, route, core):
    lane = lax.broadcasted_iota(jnp.int32, (8, 128), 1)
    named = [lane == ids[:, j : j + 1] for j in range(2)]
    hit = (named[0] | named[1]).astype(F32)
    row, col = (lax.broadcasted_iota(jnp.int32, (8, 8), d) for d in range(2))
    earlier = ((col < row) & (col // 4 == row // 4)).astype(F32)
    count = jnp.dot(earlier, hit, preferred_element_type=F32)
    here = lax.broadcasted_iota(jnp.int32, (8, 1), 0) // 4 == core
    at = lax.broadcasted_iota(jnp.int32, (64, 128), 1)
    pick, mix = None, None
    for j in range(2):
        slot = jnp.sum(jnp.where(named[j], count, 0.0), axis=1, keepdims=True).astype(jnp.int32)
        target = jnp.where(here, ids[:, j : j + 1] * 16 + slot, -64)
        mask = at == jnp.concatenate([target + 2 * k for k in range(8)], axis=0)
        weight = jnp.concatenate([route[:, j : j + 1]] * 8, axis=0)
        one = jnp.where(mask, 1.0, 0.0)
        pick = one if j == 0 else pick + one
        mix = one * weight if j == 0 else mix + one * weight
    return pick.astype(BF16), mix


def swap_fields():
    row, col = (lax.broadcasted_iota(jnp.int32, (128, 128), d) for d in range(2))
    swapped = (row // 2 % 8) * 16 + (row // 16) * 2 + row % 2
    return jnp.where(col == swapped, 1.0, 0.0).astype(BF16)


GATHER = 14


def expert_kernel(
    gated, weight, ids, route, layer_hbm, gate_hbm, up_hbm, down_hbm,
    out,
    own, left, first, mine, got0, sums, got1, mid, got2, last, got3, residual,
    gate, up, down, message, arrived, rows, act, part, got_hop, got_full, quad, got_quad,
    reply, returned, local, ss, rs, mss, mrs,
):
    z, y, c, x = place()
    e = y * 2 + c
    sems = (ss, rs)
    mixer_sems = (mss, mrs)
    loads = []
    for i, (a, b) in enumerate(((gate_hbm, gate), (up_hbm, up), (down_hbm, down))):
        load = pltpu.make_async_copy(a.at[0], b, local.at[i])
        load.start()
        loads.append(load)
    chip_rows = pltpu.make_async_copy(
        layer_hbm.at[:, pl.ds(pl.multiple_of(y * 32, 32), 32)], own, local.at[3]
    )
    chip_rows.start()

    def dev_e(d):
        return (z, lax.rem(e + d, 8), x)

    def dev_x(d):
        return (z, e, lax.rem(x + d, 4))

    def dev_y(d):
        return (z, lax.rem(y + d, 4) * 2 + c, x)

    def dev_z(d):
        return (lax.rem(z + d, 4), e, x)

    sibling = (z, y * 2 + 1 - c, x)
    friends = [dev_e(d) for d in range(1, 8)] + [f(d) for f in (dev_x, dev_z) for d in (1, 2, 3)]
    barrier = pltpu.get_barrier_semaphore()
    for friend in friends:
        pl.semaphore_signal(barrier, inc=1, device_id=friend, device_id_type=MESH)

    MIXER = 15
    other = 1 - c

    def product(s, half, q):
        cols = pl.ds(pl.multiple_of(half * 2048 + q * 1024, 1024), 1024)
        return jnp.dot(left[s], weight[:, cols], preferred_element_type=F32)

    def mixer_swap(s):
        copies = []
        for q in range(2):
            copy = remote(first.at[s, q], got0.at[s, q], mixer_sems, s * MIXER + q, sibling)
            copy.start()
            copies.append(copy)
        return copies

    def mixer_first(s, swaps):
        copies = []
        for q in range(2):
            swaps[q].wait()
            both = (mine[s, q] + got0[s, q].astype(F32)).reshape(4, 4, 8, 1024)
            both = jnp.concatenate([both[..., :512], both[..., 512:]], axis=2).astype(BF16)
            if q == 0:
                for at in range(4):
                    for to in range(4):
                        sums[s, q, to, at] = both[at, to]
            else:
                sums[s, q] = both
            dev, at = (dev_x, x) if q == 0 else (dev_y, y)
            for d in (1, 2, 3):
                copy = remote(
                    sums.at[s, q, lax.rem(at + d, 4)],
                    got1.at[s, q, d - 1],
                    mixer_sems,
                    s * MIXER + 2 + q * 3 + d - 1,
                    dev(d),
                )
                copy.start()
                copies.append(copy)
        return copies

    def mixer_second(s, ones):
        copies = []
        for q in range(2):
            for copy in ones[q * 3 : q * 3 + 3]:
                copy.wait()
            total = sums[s, q, x if q == 0 else y].astype(F32)
            for d in range(3):
                total = total + got1[s, q, d].astype(F32)
            mid[s, q] = total.astype(BF16)
            dev, at = (dev_y, y) if q == 0 else (dev_x, x)
            for d in (1, 2, 3):
                copy = remote(
                    mid.at[s, q, lax.rem(at + d, 4)],
                    got2.at[s, q, d - 1],
                    mixer_sems,
                    s * MIXER + 8 + q * 3 + d - 1,
                    dev(d),
                )
                copy.start()
                copies.append(copy)
        return copies

    def mixer_third(s, twos):
        for q in range(2):
            for copy in twos[q * 3 : q * 3 + 3]:
                copy.wait()
            total = mid[s, q, y if q == 0 else x].astype(F32)
            for d in range(3):
                total = total + got2[s, q, d].astype(F32)
            last[s, q] = total
        copy = remote(last.at[s], got3.at[s], mixer_sems, s * MIXER + 14, sibling)
        copy.start()
        return copy

    picks, mixes = [], []
    for s in range(2):
        pick, mix = tables(
            jnp.concatenate([ids[s]] * 2, axis=0), jnp.concatenate([route[s]] * 2, axis=0), c
        )
        picks.append(pick)
        mixes.append(mix)
    swap = swap_fields()

    sends = {}

    row, col = (lax.broadcasted_iota(jnp.int32, (16, 32), d) for d in range(2))
    chosen = jnp.where(col == row // 4 * 16 + x * 4 + row % 4, 1.0, 0.0).astype(BF16)

    def rows_out(s, copy):
        if s == 0:
            chip_rows.wait()
        for half, source in ((c, last), (other, got3)):
            if source is got3:
                copy.wait()
            for q in range(2):
                for k in range(2):
                    cols = pl.ds(pl.multiple_of(half * 2048 + q * 1024 + k * 512, 512), 512)
                    step_rows = jnp.dot(chosen, own[s, :, cols], preferred_element_type=F32)
                    residual[s, :, cols] = source[s, q, k * 8 : k * 8 + 8] + step_rows[:8]
        value = residual[s]
        normed = value * lax.rsqrt(jnp.mean(value * value, axis=-1, keepdims=True) + 1e-06)
        stacked = jnp.concatenate([normed[:, k * 512 : (k + 1) * 512] for k in range(8)], axis=0)
        spread_rows = lax.dot_general(
            picks[s], stacked.astype(BF16), (((0,), (0,)), ((), ())), preferred_element_type=F32
        )
        message[s] = spread_rows.astype(BF16).reshape(8, 16, 512)
        for d in range(1, 8):
            copy = remote(
                message.at[s, lax.rem(e + d, 8)],
                arrived.at[s, e],
                sems,
                s * 7 + d - 1,
                dev_e(d),
            )
            copy.start()
            sends[s, d] = copy
        arrived[s, e] = message[s, e]

    base = 14
    halves = (pl.ds(0, 2048), pl.ds(2048, 2048))

    def first_gather(s):
        for d in range(1, 8):
            sends[s, d].wait()
        ordered = jnp.dot(
            swap, arrived[s].reshape(128, 512), preferred_element_type=F32
        ).astype(BF16)
        for k in range(8):
            h, at = divmod(k, 4)
            rows[s, h, z, x, :, at * 512 : (at + 1) * 512] = ordered[k * 16 : (k + 1) * 16]
        copies = []
        for h in range(2):
            for d in (1, 2, 3):
                copy = remote(
                    rows.at[s, h, z, x],
                    rows.at[s, h, z, x],
                    sems,
                    base + s * GATHER + h * 3 + d - 1,
                    (dev_x if h == 0 else dev_z)(d),
                )
                copy.start()
                copies.append(copy)
        return copies

    def band(s, h, at, half=None):
        along = pl.ds(0, 4) if half is None else pl.ds(2 * half, 2)
        return rows.at[s, h, at, along] if h == 0 else rows.at[s, h, along, at]

    def second_gather(s, firsts):
        copies = []
        at0 = base + s * GATHER + 6
        for h in range(2):
            for copy in firsts[h * 3 : h * 3 + 3]:
                copy.wait()
            dev, at = (dev_z, z) if h == 0 else (dev_x, x)
            for i, d in enumerate((1, 3)):
                copy = remote(band(s, h, at), band(s, h, at), sems, at0 + h * 4 + i, dev(d))
                copy.start()
                copies.append(copy)
        return copies

    def third_gather(s, seconds):
        copies = []
        at0 = base + s * GATHER + 6
        for h in range(2):
            dev, at = (dev_z, z) if h == 0 else (dev_x, x)
            for i, d in enumerate((1, 3)):
                seconds[h * 2 + i].wait()
                source = lax.rem(at + 4 - d, 4)
                copy = remote(
                    band(s, h, source, i), band(s, h, source, i), sems, at0 + h * 4 + 2 + i, dev(d)
                )
                copy.start()
                copies.append(copy)
        return copies

    def compute(s):
        wide = 256

        def hidden(t, carry):
            at = pl.ds(pl.multiple_of(t * wide, wide), wide)
            g = jnp.zeros((256, wide), F32)
            u = jnp.zeros((256, wide), F32)
            for h in range(2):
                piece = rows[s, h].reshape(256, 2048)
                nt = (((1,), (1,)), ((), ()))
                g = g + lax.dot_general(piece, gate[at, halves[h]], nt, preferred_element_type=F32)
                u = u + lax.dot_general(piece, up[at, halves[h]], nt, preferred_element_type=F32)
            act[:, at] = (g / (1.0 + jnp.exp(-g)) * u).astype(BF16)
            return carry

        lax.fori_loop(0, 512 // wide, hidden, 0)

    def project(s, q):
        for h in range(2):
            from_ = slice(h * 2048 + q * 1024, h * 2048 + (q + 1) * 1024)
            value = jnp.dot(act[...], down[:, from_], preferred_element_type=F32)
            part[s, h, q] = value.astype(BF16).reshape(4, 4, 16, 1024)

    base2 = base + 2 * GATHER

    def pband(s, h, q, at, half=None):
        along = pl.ds(0, 4) if half is None else pl.ds(2 * half, 2)
        return part.at[s, h, q, at, along] if h == 0 else part.at[s, h, q, along, at]

    def first_reduce(s, q):
        copies = []
        for h in range(2):
            dev, at = (dev_z, z) if h == 0 else (dev_x, x)
            far = lax.rem(at + 2, 4)
            for i, d in enumerate((1, 3)):
                copy = remote(
                    pband(s, h, q, far, i),
                    got_hop.at[s, h, q, i],
                    sems,
                    base2 + (s * 2 + q) * GATHER + h * 4 + i,
                    dev(d),
                )
                copy.start()
                copies.append(copy)
        return copies

    def second_reduce(s, q, firsts):
        copies = []
        for h in range(2):
            dev, at = (dev_z, z) if h == 0 else (dev_x, x)
            for i, d in enumerate((1, 3)):
                firsts[h * 2 + i].wait()
                to = lax.rem(at + d, 4)
                for j in range(2):
                    k = (to, 2 * i + j) if h == 0 else (2 * i + j, to)
                    value = part[s, h, q, k[0], k[1]].astype(F32)
                    part[s, h, q, k[0], k[1]] = (
                        value + got_hop[s, h, q, i, j].astype(F32)
                    ).astype(BF16)
                copy = remote(
                    pband(s, h, q, to),
                    got_full.at[s, h, q, i],
                    sems,
                    base2 + (s * 2 + q) * GATHER + h * 4 + 2 + i,
                    dev(d),
                )
                copy.start()
                copies.append(copy)
        return copies

    def third_reduce(s, q, seconds):
        copies = []
        for h in range(2):
            for i in range(2):
                seconds[h * 2 + i].wait()
            for j in range(4):
                kept = part[s, h, q, z, j] if h == 0 else part[s, h, q, j, x]
                total = kept.astype(F32)
                for i in range(2):
                    total = total + got_full[s, h, q, i, j].astype(F32)
                quad[s, h, q, j] = total.astype(BF16)
            dev, at = (dev_x, x) if h == 0 else (dev_z, z)
            for d in (1, 2, 3):
                copy = remote(
                    quad.at[s, h, q, lax.rem(at + d, 4)],
                    got_quad.at[s, h, q, d - 1],
                    sems,
                    base2 + (s * 2 + q) * GATHER + 8 + h * 3 + d - 1,
                    dev(d),
                )
                copy.start()
                copies.append(copy)
        return copies

    base3 = base2 + 4 * GATHER

    def send_back(s, thirds):
        pieces = []
        for h in range(2):
            for q in range(2):
                for copy in thirds[q][h * 3 : h * 3 + 3]:
                    copy.wait()
                at = x if h == 0 else z
                total = quad[s, h, q, at].astype(F32)
                for d in range(3):
                    total = total + got_quad[s, h, q, d].astype(F32)
                total = total.astype(BF16)
                pieces.extend((total[:, :512], total[:, 512:]))
        stack = jnp.concatenate(pieces, axis=0)
        value = jnp.dot(swap, stack, preferred_element_type=F32).astype(BF16)
        reply[s] = value.reshape(8, 16, 512)
        copies = []
        for d in range(1, 8):
            copy = remote(
                reply.at[s, lax.rem(e + d, 8)],
                returned.at[s, e],
                sems,
                base3 + s * 7 + d - 1,
                dev_e(d),
            )
            copy.start()
            copies.append(copy)
        returned[s, e] = reply[s, e]
        return copies

    row, col = (lax.broadcasted_iota(jnp.int32, (128, 128), d) for d in range(2))
    moved = row // 32 * 32 + row // 4 % 2 * 16 + row // 8 % 4 * 4 + row % 4
    turn = jnp.where(col == moved, 1.0, 0.0).astype(BF16)
    for s in range(2):
        left[s] = jnp.dot(turn, gated[s], preferred_element_type=F32).astype(BF16)
        for q in range(2):
            first[s, q] = product(s, other, q).astype(BF16)
    pl.semaphore_wait(barrier, len(friends))
    swap0 = mixer_swap(0)
    swap1 = mixer_swap(1)
    for s in range(2):
        for q in range(2):
            mine[s, q] = product(s, c, q)
    ones0 = mixer_first(0, swap0)
    ones1 = mixer_first(1, swap1)
    twos0 = mixer_second(0, ones0)
    twos1 = mixer_second(1, ones1)
    last0 = mixer_third(0, twos0)
    rows_out(0, last0)
    last1 = mixer_third(1, twos1)
    first0 = first_gather(0)
    rows_out(1, last1)
    second0 = second_gather(0, first0)
    first1 = first_gather(1)
    third0 = third_gather(0, second0)
    second1 = second_gather(1, first1)
    for copy in third0:
        copy.wait()
    for load in loads[:2]:
        load.wait()
    compute(0)
    third1 = third_gather(1, second1)
    loads[2].wait()
    project(0, 0)
    hop00 = first_reduce(0, 0)
    project(0, 1)
    hop01 = first_reduce(0, 1)
    full00 = second_reduce(0, 0, hop00)
    full01 = second_reduce(0, 1, hop01)
    for copy in third1:
        copy.wait()
    compute(1)
    project(1, 0)
    hop10 = first_reduce(1, 0)
    project(1, 1)
    hop11 = first_reduce(1, 1)
    quad00 = third_reduce(0, 0, full00)
    full10 = second_reduce(1, 0, hop10)
    quad01 = third_reduce(0, 1, full01)
    full11 = second_reduce(1, 1, hop11)
    back0 = send_back(0, (quad00, quad01))
    quad10 = third_reduce(1, 0, full10)
    quad11 = third_reduce(1, 1, full11)
    back1 = send_back(1, (quad10, quad11))
    for copy in back0 + back1:
        copy.wait()
    for s in range(2):
        replies = returned[s].reshape(128, 512)
        high = mixes[s].astype(BF16)
        low = (mixes[s] - high.astype(F32)).astype(BF16)
        value = jnp.dot(high, replies, preferred_element_type=F32)
        value = value + jnp.dot(low, replies, preferred_element_type=F32)
        for k in range(8):
            cols = slice(k * 512, (k + 1) * 512)
            total = residual[s, :, cols] + value[k * 8 : (k + 1) * 8]
            out[s, :, cols] = jnp.where(c == 0, total[:4], total[4:]).astype(BF16)


def expert_layer(gated, weight, ids, route, layer_in, gate, up, down):
    vmem = pl.BlockSpec(memory_space=pltpu.VMEM)
    hbm = pl.BlockSpec(memory_space=pl.ANY)
    count = 14 + 6 * GATHER + 14
    return pl.pallas_call(
        expert_kernel,
        out_shape=jax.ShapeDtypeStruct((2, 4, 4096), BF16),
        in_specs=[vmem] * 4 + [hbm] * 4,
        out_specs=vmem,
        scratch_shapes=[
            pltpu.VMEM((2, 32, 4096), BF16),
            pltpu.VMEM((2, 128, 128), BF16),
            pltpu.VMEM((2, 2, 128, 1024), BF16),
            pltpu.VMEM((2, 2, 128, 1024), F32),
            pltpu.VMEM((2, 2, 128, 1024), BF16),
            pltpu.VMEM((2, 2, 4, 4, 16, 512), BF16),
            pltpu.VMEM((2, 2, 3, 4, 16, 512), BF16),
            pltpu.VMEM((2, 2, 4, 16, 512), BF16),
            pltpu.VMEM((2, 2, 3, 16, 512), BF16),
            pltpu.VMEM((2, 2, 16, 512), F32),
            pltpu.VMEM((2, 2, 16, 512), F32),
            pltpu.VMEM((2, 8, 4096), F32),
            pltpu.VMEM((512, 4096), BF16),
            pltpu.VMEM((512, 4096), BF16),
            pltpu.VMEM((512, 4096), BF16),
            pltpu.VMEM((2, 8, 16, 512), BF16),
            pltpu.VMEM((2, 8, 16, 512), BF16),
            pltpu.VMEM((2, 2, 4, 4, 16, 2048), BF16),
            pltpu.VMEM((256, 512), BF16),
            pltpu.VMEM((2, 2, 2, 4, 4, 16, 1024), BF16),
            pltpu.VMEM((2, 2, 2, 2, 2, 16, 1024), BF16),
            pltpu.VMEM((2, 2, 2, 2, 4, 16, 1024), BF16),
            pltpu.VMEM((2, 2, 2, 4, 16, 1024), BF16),
            pltpu.VMEM((2, 2, 2, 3, 16, 1024), BF16),
            pltpu.VMEM((2, 8, 16, 512), BF16),
            pltpu.VMEM((2, 8, 16, 512), BF16),
            pltpu.SemaphoreType.DMA((4,)),
            pltpu.SemaphoreType.DMA((count,)),
            pltpu.SemaphoreType.DMA((count,)),
            pltpu.SemaphoreType.DMA((30,)),
            pltpu.SemaphoreType.DMA((30,)),
        ],
        compiler_params=pltpu.CompilerParams(
            collective_id=1, has_side_effects=True, vmem_limit_bytes=58 * MIB
        ),
        name="experts",
    )(gated, weight, ids, route, layer_in, gate, up, down)


def shards(
    layer_in,
    conv_state,
    ssm_state,
    proj_inner,
    proj_gate,
    conv_weight,
    conv_bias,
    delta_down,
    state_proj,
    delta_up,
    delta_bias,
    decay_log,
    skip_gain,
    proj_out,
    expert_gate,
    expert_up,
    expert_down,
    expert_ids,
    route_weight,
):
    conv_in, activated, gate_branch, step_size, state_in = mixer_in(
        layer_in.reshape(256, 4096),
        proj_inner,
        proj_gate,
        jnp.transpose(conv_state, (1, 0, 2)),
        conv_weight,
        conv_bias[None],
        delta_down,
        state_proj.reshape(32, 128),
        delta_up,
        delta_bias[None],
    )
    conv_final = jnp.stack([conv_state[:, 2], conv_in[:128], conv_in[128:]], axis=1)
    step_size = step_size.reshape(2, 128, 128)
    state_in = state_in.reshape(2, 128, 32)
    rates = jnp.exp(decay_log)[None]
    act_float = activated.astype(F32).reshape(2, 128, 128)
    gate_branch = gate_branch.reshape(2, 128, 128)
    gated = []
    for s in range(2):
        size = step_size[s][:, None, :]
        ssm_state = (
            jnp.exp(-size * rates) * ssm_state
            + size * state_in[s, :, :16, None] * act_float[s][:, None, :]
        )
        readout = jnp.sum(ssm_state * state_in[s, :, 16:, None], axis=1)
        gated.append(
            ((readout + skip_gain * act_float[s]) * gate_branch[s]).astype(BF16)
        )
    layer_out = expert_layer(
        jnp.stack(gated),
        proj_out,
        expert_ids,
        route_weight,
        layer_in,
        expert_gate,
        expert_up,
        expert_down,
    )
    return (layer_out, conv_final, ssm_state)


def solution(mesh):
    channels = ("expert", "tensor")
    rows = ("dp", "expert", "tensor")
    placed = (
        P(None, "dp", None),
        P("dp", None, channels),
        P("dp", None, channels),
        P(None, channels),
        P(None, channels),
        P(None, channels),
        P(channels),
        P(channels, None),
        P(None, None, channels),
        P(None, channels),
        P(channels),
        P(None, channels),
        P(channels),
        P(channels, None),
        P("expert", ("dp", "tensor"), None),
        P("expert", ("dp", "tensor"), None),
        P("expert", ("dp", "tensor"), None),
        P(None, rows, None),
        P(None, rows, None),
    )
    return jax.shard_map(
        shards,
        mesh=mesh,
        in_specs=placed,
        out_specs=(P(None, rows, None), P("dp", None, channels), P("dp", None, channels)),
        check_vma=False,
    )
```

```python
import functools

import jax
import jax.numpy as jnp
from jax import lax
from jax.experimental import pallas as pl
from jax.experimental.pallas import tpu as pltpu
from jax.sharding import PartitionSpec as P

MESH = pl.DeviceIdType.MESH
F32 = jnp.float32
BF16 = jnp.bfloat16
MIB = 2**20


def place():
    z, e, x = lax.axis_index("dp"), lax.axis_index("expert"), lax.axis_index("tensor")
    return z, lax.div(e, 2), lax.rem(e, 2), x


def remote(src, dst, sems, at, device):
    return pltpu.make_async_remote_copy(
        src_ref=src,
        dst_ref=dst,
        send_sem=sems[0].at[at],
        recv_sem=sems[1].at[at],
        device_id=device,
        device_id_type=MESH,
    )


def greet(devices):
    barrier = pltpu.get_barrier_semaphore()
    for device in devices:
        pl.semaphore_signal(barrier, inc=1, device_id=device, device_id_type=MESH)
    pl.semaphore_wait(barrier, len(devices))


def silu(v):
    return v / (1.0 + jnp.exp(-v))


PIECES = 4


def mixer_in_kernel(
    rows_hbm, inner_hbm, gate_hbm, conv_state, conv_weight, conv_bias, delta_down, state_proj,
    delta_up, delta_bias,
    conv_out, act_out, gate_out, size_out, state_out,
    rows, inner, gate, local, part, got, both, recv, out, one, other, send_a, recv_a, send_b, recv_b,
):
    z, y, c, x = place()
    me = y * 4 + x
    width = 4096 // PIECES
    loads = []
    for k in range(PIECES):
        cut = pl.ds(k * width, width)
        three = []
        for i, (a, b) in enumerate(
            (
                (rows_hbm.at[:, cut], rows.at[:, cut]),
                (inner_hbm.at[cut], inner.at[cut]),
                (gate_hbm.at[cut], gate.at[cut]),
            )
        ):
            load = pltpu.make_async_copy(a, b, local.at[k * 3 + i])
            load.start()
            three.append(load)
        loads.append(three)

    def chip(p):
        return (z, lax.div(p, 4) * 2 + c, lax.rem(p, 4))

    sibling = (z, y * 2 + 1 - c, x)
    barrier = pltpu.get_barrier_semaphore()
    pl.semaphore_signal(barrier, inc=1, device_id=sibling, device_id_type=MESH)

    def signal(i, carry):
        pl.semaphore_signal(
            barrier, inc=1, device_id=chip(lax.rem(me + i, 16)), device_id_type=MESH
        )
        return carry

    lax.fori_loop(1, 16, signal, 0)

    squares = jnp.zeros((256, 1), F32)
    conv_in = jnp.zeros((256, 128), F32)
    for k in range(PIECES):
        loads[k][0].wait()
        loads[k][1].wait()
        piece = rows[:, k * width : (k + 1) * width]
        conv_in = conv_in + jnp.dot(
            piece, inner[k * width : (k + 1) * width], preferred_element_type=F32
        )
        wide = piece.astype(F32)
        squares = squares + jnp.sum(wide * wide, axis=1, keepdims=True)
    scale = lax.rsqrt(squares * (1.0 / 4096) + 1e-06)
    conv_in = (conv_in * scale).astype(BF16)
    conv_out[0] = conv_state[2]
    conv_out[1] = conv_in[:128]
    conv_out[2] = conv_in[128:]
    conv_in = conv_in.astype(F32)
    window = [conv_state[k].astype(F32) for k in range(3)] + [conv_in[:128], conv_in[128:]]
    acts = []
    for s in range(2):
        total = conv_bias[...]
        for k in range(4):
            total = total + window[s + k] * conv_weight[k : k + 1]
        acts.append(silu(total))
    activated = jnp.concatenate(acts, axis=0).astype(BF16)
    act_out[...] = activated
    delta = jnp.dot(activated, delta_down[...], preferred_element_type=F32)
    state = lax.dot_general(
        activated, state_proj[...], (((1,), (1,)), ((), ())), preferred_element_type=F32
    )
    state = jnp.concatenate([state, jnp.zeros((256, 224), F32)], axis=1)
    blocks = jnp.concatenate([delta.reshape(32, 8, 256), state.reshape(32, 8, 256)], axis=1)
    part[...] = blocks.astype(BF16).reshape(2, 16, 16, 256)

    pl.semaphore_wait(barrier, 16)
    swap = remote(part.at[1 - c], got, (one, other), 0, sibling)
    swap.start()
    swap.wait()
    both[...] = (part[c].astype(F32) + got[...].astype(F32)).astype(BF16)

    def first(i):
        p = lax.rem(me + i, 16)
        return remote(both.at[p], recv.at[i - 1], (send_a, recv_a), i - 1, chip(p))

    def start_first(i, carry):
        first(i).start()
        return carry

    lax.fori_loop(1, 16, start_first, 0)

    gated = jnp.zeros((256, 128), F32)
    for k in range(PIECES):
        loads[k][2].wait()
        gated = gated + jnp.dot(
            rows[:, k * width : (k + 1) * width],
            gate[k * width : (k + 1) * width],
            preferred_element_type=F32,
        )
    gate_out[...] = silu(gated * scale)

    def add(i, total):
        first(i).wait()
        return total + recv[i - 1].astype(F32)

    total = lax.fori_loop(1, 16, add, both[me].astype(F32))
    low, state = total[:8], total[8:]
    normed = low * lax.rsqrt(jnp.mean(low * low, axis=-1, keepdims=True) + 1e-06)
    high = state.astype(BF16).astype(F32)
    rest = state - high
    split = jnp.concatenate([high[:, :32], rest[:, :32], state[:, 64:]], axis=1)
    out[c, me] = jnp.concatenate([normed, split], axis=0).astype(BF16)

    def second(i):
        return remote(
            out.at[c, me], out.at[c, me], (send_b, recv_b), i - 1, chip(lax.rem(me + i, 16))
        )

    def second_from(i):
        p = lax.rem(me + 16 - i, 16)
        return remote(out.at[c, p], out.at[c, p], (send_b, recv_b), i - 1, chip(p))

    def start_second(i, carry):
        second(i).start()
        return carry

    lax.fori_loop(1, 16, start_second, 0)

    def wait_second(i, carry):
        second(i).wait_send()
        second_from(i).wait_recv()
        return carry

    lax.fori_loop(1, 16, wait_second, 0)
    swap = remote(out.at[c], out.at[c], (one, other), 1, sibling)
    swap.start()
    swap.wait_send()
    remote(out.at[1 - c], out.at[1 - c], (one, other), 1, sibling).wait_recv()
    summed = out[...].reshape(32, 16, 256).astype(F32)
    normed = summed[:, :8].reshape(256, 256).astype(BF16)
    value = jnp.dot(normed, delta_up[...], preferred_element_type=F32) + delta_bias[...]
    size_out[...] = jnp.maximum(value, 0.0) + jnp.log1p(jnp.exp(-jnp.abs(value)))
    state = summed[:, 8:].reshape(256, 256)
    state_out[...] = state[:, :64].astype(BF16)


def mixer_in(rows, inner, gate, *rest):
    vmem = pl.BlockSpec(memory_space=pltpu.VMEM)
    hbm = pl.BlockSpec(memory_space=pl.ANY)
    return pl.pallas_call(
        mixer_in_kernel,
        out_shape=(
            jax.ShapeDtypeStruct((3, 128, 128), BF16),
            jax.ShapeDtypeStruct((256, 128), BF16),
            jax.ShapeDtypeStruct((256, 128), F32),
            jax.ShapeDtypeStruct((256, 128), F32),
            jax.ShapeDtypeStruct((256, 64), BF16),
        ),
        in_specs=[hbm] * 3 + [vmem] * len(rest),
        out_specs=(vmem,) * 5,
        scratch_shapes=[
            pltpu.VMEM((256, 4096), BF16),
            pltpu.VMEM((4096, 128), BF16),
            pltpu.VMEM((4096, 128), BF16),
            pltpu.SemaphoreType.DMA((3 * PIECES,)),
            pltpu.VMEM((2, 16, 16, 256), BF16),
            pltpu.VMEM((16, 16, 256), BF16),
            pltpu.VMEM((16, 16, 256), BF16),
            pltpu.VMEM((15, 16, 256), BF16),
            pltpu.VMEM((2, 16, 16, 256), BF16),
            pltpu.SemaphoreType.DMA((2,)),
            pltpu.SemaphoreType.DMA((2,)),
            pltpu.SemaphoreType.DMA((15,)),
            pltpu.SemaphoreType.DMA((15,)),
            pltpu.SemaphoreType.DMA((15,)),
            pltpu.SemaphoreType.DMA((15,)),
        ],
        compiler_params=pltpu.CompilerParams(
            collective_id=0, has_side_effects=True, vmem_limit_bytes=56 * MIB
        ),
        name="mixer_in",
    )(rows, inner, gate, *rest)


BLOCK = 32


def recurrence_kernel(size, act, gate, state_in, decay_log, skip, before, gated, after):
    rates = jnp.exp(decay_log[...])[None]
    held = before[...]
    long = BLOCK * 16
    row, col = (lax.broadcasted_iota(jnp.int32, (long, BLOCK), d) for d in range(2))
    copy = jnp.where(row // 16 == col, 1.0, 0.0).astype(BF16)
    row, col = (lax.broadcasted_iota(jnp.int32, (long, 64), d) for d in range(2))
    masks = [jnp.where(col % 32 == k * 16 + row % 16, 1.0, 0.0) for k in range(2)]
    ones = jnp.ones((64, 128), BF16)
    for s in range(2):
        spread = jnp.dot(copy, state_in[s], preferred_element_type=F32)
        b_in, c_out = (
            jnp.dot((spread * m).astype(BF16), ones, preferred_element_type=F32).reshape(
                BLOCK, 16, 128
            )
            for m in masks
        )
        step = size[s]
        x = act[s].astype(F32)
        held = (
            jnp.exp(-step[:, None, :] * rates) * held + (step * x)[:, None, :] * b_in
        )
        readout = jnp.sum(held * c_out, axis=1)
        gated[s] = ((readout + skip[...] * x) * gate[s]).astype(BF16)
    after[...] = held


def recurrence(size, act, gate, state_in, decay_log, skip, before):
    rows = pl.BlockSpec((2, BLOCK, 128), lambda i: (0, i, 0))
    state = pl.BlockSpec((BLOCK, 16, 128), lambda i: (i, 0, 0))
    return pl.pallas_call(
        recurrence_kernel,
        grid=(128 // BLOCK,),
        out_shape=(
            jax.ShapeDtypeStruct((2, 128, 128), BF16),
            jax.ShapeDtypeStruct((128, 16, 128), F32),
        ),
        in_specs=[
            rows,
            rows,
            rows,
            pl.BlockSpec((2, BLOCK, 64), lambda i: (0, i, 0)),
            pl.BlockSpec((16, 128), lambda i: (0, 0)),
            pl.BlockSpec((1, 128), lambda i: (0, 0)),
            state,
        ],
        out_specs=(rows, state),
        compiler_params=pltpu.CompilerParams(vmem_limit_bytes=60 * MIB),
        name="recurrence",
    )(size, act, gate, state_in, decay_log, skip, before)


def tables(ids, route, core):
    row, col = (lax.broadcasted_iota(jnp.int32, (8, 4), d) for d in range(2))
    own = row % 4 == col
    ids, route = (
        [jnp.sum(jnp.where(own, v[j : j + 1], 0), axis=1, keepdims=True) for j in range(2)]
        for v in (ids, route)
    )
    lane = lax.broadcasted_iota(jnp.int32, (8, 128), 1)
    named = [lane == ids[j] for j in range(2)]
    hit = (named[0] | named[1]).astype(F32)
    row, col = (lax.broadcasted_iota(jnp.int32, (8, 8), d) for d in range(2))
    earlier = ((col < row) & (col // 4 == row // 4)).astype(F32)
    count = jnp.dot(earlier, hit, preferred_element_type=F32)
    here = lax.broadcasted_iota(jnp.int32, (8, 1), 0) // 4 == core
    at = lax.broadcasted_iota(jnp.int32, (64, 128), 1)
    pick, mix = None, None
    for j in range(2):
        slot = jnp.sum(jnp.where(named[j], count, 0.0), axis=1, keepdims=True).astype(jnp.int32)
        target = jnp.where(here, ids[j] * 16 + slot, -64)
        mask = at == jnp.concatenate([target + 2 * k for k in range(8)], axis=0)
        weight = jnp.concatenate([route[j]] * 8, axis=0)
        one = jnp.where(mask, 1.0, 0.0)
        pick = one if j == 0 else pick + one
        mix = one * weight if j == 0 else mix + one * weight
    return pick.astype(BF16), mix


def swap_fields():
    row, col = (lax.broadcasted_iota(jnp.int32, (128, 128), d) for d in range(2))
    swapped = (row // 2 % 8) * 16 + (row // 16) * 2 + row % 2
    return jnp.where(col == swapped, 1.0, 0.0).astype(BF16)


GATHER = 22
REDUCE = 14


def expert_kernel(
    gated, weight, ids, route, layer_hbm, gate_hbm, up_hbm, down_hbm,
    out,
    own, left, first, mine, got0, sums, got1, mid, got2, last, got3, residual,
    gate, up, down, message, arrived, rows, act, part, got_hop, got_full, quad, got_quad,
    reply, returned, local, ss, rs, mss, mrs,
):
    z, y, c, x = place()
    e = y * 2 + c
    sems = (ss, rs)
    mixer_sems = (mss, mrs)
    chip_rows = pltpu.make_async_copy(
        layer_hbm.at[:, pl.ds(pl.multiple_of(y * 32, 32), 32)], own, local.at[3]
    )
    chip_rows.start()

    def dev_e(d):
        return (z, lax.rem(e + d, 8), x)

    def dev_x(d):
        return (z, e, lax.rem(x + d, 4))

    def dev_y(d):
        return (z, lax.rem(y + d, 4) * 2 + c, x)

    def dev_z(d):
        return (lax.rem(z + d, 4), e, x)

    sibling = (z, y * 2 + 1 - c, x)
    friends = [dev_e(d) for d in range(1, 8)] + [f(d) for f in (dev_x, dev_z) for d in (1, 2, 3)]
    barrier = pltpu.get_barrier_semaphore()
    for friend in friends:
        pl.semaphore_signal(barrier, inc=1, device_id=friend, device_id_type=MESH)

    MIXER = 15
    other = 1 - c

    def product(s, half, q):
        cols = pl.ds(pl.multiple_of(half * 2048 + q * 1024, 1024), 1024)
        return jnp.dot(left[s], weight[:, cols], preferred_element_type=F32)

    def mixer_swap(s):
        copies = []
        for q in range(2):
            copy = remote(first.at[s, q], got0.at[s, q], mixer_sems, s * MIXER + q, sibling)
            copy.start()
            copies.append(copy)
        return copies

    def mixer_first(s, swaps):
        copies = []
        for q in range(2):
            swaps[q].wait()
            both = (mine[s, q] + got0[s, q].astype(F32)).reshape(4, 4, 8, 1024)
            both = jnp.concatenate([both[..., :512], both[..., 512:]], axis=2).astype(BF16)
            if q == 0:
                for at in range(4):
                    for to in range(4):
                        sums[s, q, to, at] = both[at, to]
            else:
                sums[s, q] = both
            dev, at = (dev_x, x) if q == 0 else (dev_y, y)
            for d in (1, 2, 3):
                copy = remote(
                    sums.at[s, q, lax.rem(at + d, 4)],
                    got1.at[s, q, d - 1],
                    mixer_sems,
                    s * MIXER + 2 + q * 3 + d - 1,
                    dev(d),
                )
                copy.start()
                copies.append(copy)
        return copies

    def mixer_second(s, ones):
        copies = []
        for q in range(2):
            for copy in ones[q * 3 : q * 3 + 3]:
                copy.wait()
            total = sums[s, q, x if q == 0 else y].astype(F32)
            for d in range(3):
                total = total + got1[s, q, d].astype(F32)
            mid[s, q] = total.astype(BF16)
            dev, at = (dev_y, y) if q == 0 else (dev_x, x)
            for d in (1, 2, 3):
                copy = remote(
                    mid.at[s, q, lax.rem(at + d, 4)],
                    got2.at[s, q, d - 1],
                    mixer_sems,
                    s * MIXER + 8 + q * 3 + d - 1,
                    dev(d),
                )
                copy.start()
                copies.append(copy)
        return copies

    def mixer_third(s, twos):
        for q in range(2):
            for copy in twos[q * 3 : q * 3 + 3]:
                copy.wait()
            total = mid[s, q, y if q == 0 else x].astype(F32)
            for d in range(3):
                total = total + got2[s, q, d].astype(F32)
            last[s, q] = total
        copy = remote(last.at[s], got3.at[s], mixer_sems, s * MIXER + 14, sibling)
        copy.start()
        return copy

    picks, mixes, helpers, sends = [], [], [], {}

    def rows_out(s, copy):
        if s == 0:
            chip_rows.wait()
        for half, source in ((c, last), (other, got3)):
            if source is got3:
                copy.wait()
            for q in range(2):
                for k in range(2):
                    cols = pl.ds(pl.multiple_of(half * 2048 + q * 1024 + k * 512, 512), 512)
                    step_rows = jnp.dot(helpers[1], own[s, :, cols], preferred_element_type=F32)
                    residual[s, :, cols] = source[s, q, k * 8 : k * 8 + 8] + step_rows[:8]
        value = residual[s]
        normed = value * lax.rsqrt(jnp.mean(value * value, axis=-1, keepdims=True) + 1e-06)
        stacked = jnp.concatenate([normed[:, k * 512 : (k + 1) * 512] for k in range(8)], axis=0)
        spread_rows = lax.dot_general(
            picks[s], stacked.astype(BF16), (((0,), (0,)), ((), ())), preferred_element_type=F32
        )
        message[s] = spread_rows.astype(BF16).reshape(8, 16, 512)
        for d in range(1, 8):
            copy = remote(
                message.at[s, lax.rem(e + d, 8)],
                arrived.at[s, e],
                sems,
                s * 7 + d - 1,
                dev_e(d),
            )
            copy.start()
            sends[s, d] = copy
        arrived[s, e] = message[s, e]

    base = 14
    halves = (slice(0, 2048), slice(2048, 4096))

    def first_gather(s):
        for d in range(1, 8):
            sends[s, d].wait()
        ordered = jnp.dot(
            helpers[0], arrived[s].reshape(128, 512), preferred_element_type=F32
        ).astype(BF16)
        for k in range(8):
            h, at = divmod(k, 4)
            rows[s, h, z, x, :, at * 512 : (at + 1) * 512] = ordered[k * 16 : (k + 1) * 16]
        copies = []
        for h in range(2):
            for d in (1, 2, 3):
                copy = remote(
                    rows.at[s, h, z, x],
                    rows.at[s, h, z, x],
                    sems,
                    base + s * GATHER + h * 3 + d - 1,
                    (dev_x if h == 0 else dev_z)(d),
                )
                copy.start()
                copies.append(copy)
        return copies

    def band(s, h, q, at, half=None):
        along = pl.ds(0, 4) if half is None else pl.ds(2 * half, 2)
        every, cols = slice(None), pl.ds(q * 1024, 1024)
        at = (at, along) if h == 0 else (along, at)
        return rows.at[(s, h, *at, every, cols)]

    def second_gather(s, firsts):
        copies = {}
        for q in range(2):
            for h in range(2):
                if q == 0:
                    for copy in firsts[h * 3 : h * 3 + 3]:
                        copy.wait()
                dev, at = (dev_z, z) if h == 0 else (dev_x, x)
                for i, d in enumerate((1, 3)):
                    mine_ = band(s, h, q, at)
                    n = base + s * GATHER + 6 + q * 8 + h * 4 + i
                    copy = remote(mine_, mine_, sems, n, dev(d))
                    copy.start()
                    copies[q, h, i] = copy
        return copies

    def third_gather(s, q, seconds):
        copies = []
        for h in range(2):
            dev, at = (dev_z, z) if h == 0 else (dev_x, x)
            for i, d in enumerate((1, 3)):
                seconds[q, h, i].wait()
                piece = band(s, h, q, lax.rem(at + 4 - d, 4), i)
                n = base + s * GATHER + 6 + q * 8 + h * 4 + 2 + i
                copy = remote(piece, piece, sems, n, dev(d))
                copy.start()
                copies.append(copy)
        return copies

    def compute(s, t):
        at = slice(t * 256, (t + 1) * 256)
        g = jnp.zeros((256, 256), F32)
        u = jnp.zeros((256, 256), F32)
        for h in range(2):
            piece = rows[s, h].reshape(256, 2048)
            nt = (((1,), (1,)), ((), ()))
            g = g + lax.dot_general(piece, gate[at, halves[h]], nt, preferred_element_type=F32)
            u = u + lax.dot_general(piece, up[at, halves[h]], nt, preferred_element_type=F32)
        act[:, at] = (silu(g) * u).astype(BF16)

    def project(s, q):
        for h in range(2):
            from_ = slice(h * 2048 + q * 1024, h * 2048 + (q + 1) * 1024)
            value = jnp.dot(act[...], down[:, from_], preferred_element_type=F32)
            part[s, h, q] = value.astype(BF16).reshape(4, 4, 16, 1024)

    base2 = base + 2 * GATHER

    def pband(s, h, q, at, half=None):
        along = pl.ds(0, 4) if half is None else pl.ds(2 * half, 2)
        return part.at[s, h, q, at, along] if h == 0 else part.at[s, h, q, along, at]

    def first_reduce(s, q):
        copies = []
        for h in range(2):
            dev, at = (dev_z, z) if h == 0 else (dev_x, x)
            far = lax.rem(at + 2, 4)
            for i, d in enumerate((1, 3)):
                copy = remote(
                    pband(s, h, q, far, i),
                    got_hop.at[s, h, q, i],
                    sems,
                    base2 + (s * 2 + q) * REDUCE + h * 4 + i,
                    dev(d),
                )
                copy.start()
                copies.append(copy)
        return copies

    def second_reduce(s, q, firsts):
        copies = []
        for h in range(2):
            dev, at = (dev_z, z) if h == 0 else (dev_x, x)
            for i, d in enumerate((1, 3)):
                firsts[h * 2 + i].wait()
                to = lax.rem(at + d, 4)
                for j in range(2):
                    k = (to, 2 * i + j) if h == 0 else (2 * i + j, to)
                    value = part[s, h, q, k[0], k[1]].astype(F32)
                    part[s, h, q, k[0], k[1]] = (
                        value + got_hop[s, h, q, i, j].astype(F32)
                    ).astype(BF16)
                copy = remote(
                    pband(s, h, q, to),
                    got_full.at[s, h, q, i],
                    sems,
                    base2 + (s * 2 + q) * REDUCE + h * 4 + 2 + i,
                    dev(d),
                )
                copy.start()
                copies.append(copy)
        return copies

    def third_reduce(s, q, seconds):
        copies = []
        for h in range(2):
            for i in range(2):
                seconds[h * 2 + i].wait()
            for j in range(4):
                kept = part[s, h, q, z, j] if h == 0 else part[s, h, q, j, x]
                total = kept.astype(F32)
                for i in range(2):
                    total = total + got_full[s, h, q, i, j].astype(F32)
                quad[s, h, q, j] = total.astype(BF16)
            dev, at = (dev_x, x) if h == 0 else (dev_z, z)
            for d in (1, 2, 3):
                copy = remote(
                    quad.at[s, h, q, lax.rem(at + d, 4)],
                    got_quad.at[s, h, q, d - 1],
                    sems,
                    base2 + (s * 2 + q) * REDUCE + 8 + h * 3 + d - 1,
                    dev(d),
                )
                copy.start()
                copies.append(copy)
        return copies

    base3 = base2 + 4 * REDUCE

    def send_back(s, thirds):
        pieces = []
        for h in range(2):
            for q in range(2):
                for copy in thirds[q][h * 3 : h * 3 + 3]:
                    copy.wait()
                at = x if h == 0 else z
                total = quad[s, h, q, at].astype(F32)
                for d in range(3):
                    total = total + got_quad[s, h, q, d].astype(F32)
                total = total.astype(BF16)
                pieces.extend((total[:, :512], total[:, 512:]))
        stack = jnp.concatenate(pieces, axis=0)
        value = jnp.dot(helpers[0], stack, preferred_element_type=F32).astype(BF16)
        reply[s] = value.reshape(8, 16, 512)
        copies = []
        for d in range(1, 8):
            copy = remote(
                reply.at[s, lax.rem(e + d, 8)],
                returned.at[s, e],
                sems,
                base3 + s * 7 + d - 1,
                dev_e(d),
            )
            copy.start()
            copies.append(copy)
        returned[s, e] = reply[s, e]
        return copies

    row, col = (lax.broadcasted_iota(jnp.int32, (128, 128), d) for d in range(2))
    moved = row // 32 * 32 + row // 4 % 2 * 16 + row // 8 % 4 * 4 + row % 4
    turn = jnp.where(col == moved, 1.0, 0.0).astype(BF16)
    swaps = []
    for s in range(2):
        left[s] = jnp.dot(turn, gated[s], preferred_element_type=F32).astype(BF16)
        for q in range(2):
            first[s, q] = product(s, other, q).astype(BF16)
        if s == 0:
            pl.semaphore_wait(barrier, len(friends))
        swaps.append(mixer_swap(s))
    for s in range(2):
        for q in range(2):
            mine[s, q] = product(s, c, q)
    ones0 = mixer_first(0, swaps[0])
    ones1 = mixer_first(1, swaps[1])
    for s in range(2):
        pick, mix = tables(ids[s], route[s], c)
        picks.append(pick)
        mixes.append(mix)
    swap = swap_fields()
    row, col = (lax.broadcasted_iota(jnp.int32, (16, 32), d) for d in range(2))
    chosen = jnp.where(col == row // 4 * 16 + x * 4 + row % 4, 1.0, 0.0).astype(BF16)
    helpers.extend((swap, chosen))
    loads = []
    for i, (a, b) in enumerate(((gate_hbm, gate), (up_hbm, up), (down_hbm, down))):
        load = pltpu.make_async_copy(a.at[0], b, local.at[i])
        load.start()
        loads.append(load)
    twos0 = mixer_second(0, ones0)
    twos1 = mixer_second(1, ones1)
    last0 = mixer_third(0, twos0)
    rows_out(0, last0)
    last1 = mixer_third(1, twos1)
    first0 = first_gather(0)
    rows_out(1, last1)
    second0 = second_gather(0, first0)
    first1 = first_gather(1)
    third00 = third_gather(0, 0, second0)
    third01 = third_gather(0, 1, second0)
    second1 = second_gather(1, first1)
    for copy in third00 + third01:
        copy.wait()
    for load in loads[:2]:
        load.wait()
    compute(0, 0)
    third10 = third_gather(1, 0, second1)
    compute(0, 1)
    loads[2].wait()
    project(0, 0)
    hop00 = first_reduce(0, 0)
    third11 = third_gather(1, 1, second1)
    project(0, 1)
    hop01 = first_reduce(0, 1)
    full00 = second_reduce(0, 0, hop00)
    full01 = second_reduce(0, 1, hop01)
    for copy in third10 + third11:
        copy.wait()
    compute(1, 0)
    compute(1, 1)
    project(1, 0)
    hop10 = first_reduce(1, 0)
    quad00 = third_reduce(0, 0, full00)
    project(1, 1)
    hop11 = first_reduce(1, 1)
    quad01 = third_reduce(0, 1, full01)
    full10 = second_reduce(1, 0, hop10)
    full11 = second_reduce(1, 1, hop11)
    back0 = send_back(0, (quad00, quad01))
    quad10 = third_reduce(1, 0, full10)
    quad11 = third_reduce(1, 1, full11)
    back1 = send_back(1, (quad10, quad11))
    for copy in back0 + back1:
        copy.wait()
    for s in range(2):
        replies = returned[s].reshape(128, 512)
        high = mixes[s].astype(BF16)
        low = (mixes[s] - high.astype(F32)).astype(BF16)
        value = jnp.dot(high, replies, preferred_element_type=F32)
        value = value + jnp.dot(low, replies, preferred_element_type=F32)
        for k in range(8):
            cols = slice(k * 512, (k + 1) * 512)
            total = residual[s, :, cols] + value[k * 8 : (k + 1) * 8]
            out[s, :, cols] = jnp.where(c == 0, total[:4], total[4:])


def expert_layer(gated, weight, ids, route, layer_in, gate, up, down):
    vmem = pl.BlockSpec(memory_space=pltpu.VMEM)
    hbm = pl.BlockSpec(memory_space=pl.ANY)
    count = 14 + 2 * GATHER + 4 * REDUCE + 14
    return pl.pallas_call(
        expert_kernel,
        out_shape=jax.ShapeDtypeStruct((2, 4, 4096), F32),
        in_specs=[vmem] * 4 + [hbm] * 4,
        out_specs=vmem,
        scratch_shapes=[
            pltpu.VMEM((2, 32, 4096), BF16),
            pltpu.VMEM((2, 128, 128), BF16),
            pltpu.VMEM((2, 2, 128, 1024), BF16),
            pltpu.VMEM((2, 2, 128, 1024), F32),
            pltpu.VMEM((2, 2, 128, 1024), BF16),
            pltpu.VMEM((2, 2, 4, 4, 16, 512), BF16),
            pltpu.VMEM((2, 2, 3, 4, 16, 512), BF16),
            pltpu.VMEM((2, 2, 4, 16, 512), BF16),
            pltpu.VMEM((2, 2, 3, 16, 512), BF16),
            pltpu.VMEM((2, 2, 16, 512), F32),
            pltpu.VMEM((2, 2, 16, 512), F32),
            pltpu.VMEM((2, 8, 4096), F32),
            pltpu.VMEM((512, 4096), BF16),
            pltpu.VMEM((512, 4096), BF16),
            pltpu.VMEM((512, 4096), BF16),
            pltpu.VMEM((2, 8, 16, 512), BF16),
            pltpu.VMEM((2, 8, 16, 512), BF16),
            pltpu.VMEM((2, 2, 4, 4, 16, 2048), BF16),
            pltpu.VMEM((256, 512), BF16),
            pltpu.VMEM((2, 2, 2, 4, 4, 16, 1024), BF16),
            pltpu.VMEM((2, 2, 2, 2, 2, 16, 1024), BF16),
            pltpu.VMEM((2, 2, 2, 2, 4, 16, 1024), BF16),
            pltpu.VMEM((2, 2, 2, 4, 16, 1024), BF16),
            pltpu.VMEM((2, 2, 2, 3, 16, 1024), BF16),
            pltpu.VMEM((2, 8, 16, 512), BF16),
            pltpu.VMEM((2, 8, 16, 512), BF16),
            pltpu.SemaphoreType.DMA((4,)),
            pltpu.SemaphoreType.DMA((count,)),
            pltpu.SemaphoreType.DMA((count,)),
            pltpu.SemaphoreType.DMA((30,)),
            pltpu.SemaphoreType.DMA((30,)),
        ],
        compiler_params=pltpu.CompilerParams(
            collective_id=1, has_side_effects=True, vmem_limit_bytes=58 * MIB
        ),
        name="experts",
    )(gated, weight, ids, route, layer_in, gate, up, down)


def shards(
    layer_in,
    conv_state,
    ssm_state,
    proj_inner,
    proj_gate,
    conv_weight,
    conv_bias,
    delta_down,
    state_proj,
    delta_up,
    delta_bias,
    decay_log,
    skip_gain,
    proj_out,
    expert_gate,
    expert_up,
    expert_down,
    expert_ids,
    route_weight,
):
    conv_final, activated, gate_branch, step_size, state_in = mixer_in(
        layer_in.reshape(256, 4096),
        proj_inner,
        proj_gate,
        jnp.transpose(conv_state, (1, 0, 2)),
        conv_weight,
        conv_bias[None],
        delta_down,
        state_proj.reshape(32, 128),
        delta_up,
        delta_bias[None],
    )
    conv_final = jnp.transpose(conv_final, (1, 0, 2))
    gated, ssm_state = recurrence(
        step_size.reshape(2, 128, 128),
        activated.reshape(2, 128, 128),
        gate_branch.reshape(2, 128, 128),
        state_in.reshape(2, 128, 64),
        decay_log,
        skip_gain[None],
        ssm_state,
    )
    layer_out = expert_layer(
        gated,
        proj_out,
        jnp.transpose(expert_ids, (0, 2, 1)),
        jnp.transpose(route_weight, (0, 2, 1)),
        layer_in,
        expert_gate,
        expert_up,
        expert_down,
    )
    return (layer_out.astype(BF16), conv_final, ssm_state)


def solution(mesh):
    channels = ("expert", "tensor")
    rows = ("dp", "expert", "tensor")
    placed = (
        P(None, "dp", None),
        P("dp", None, channels),
        P("dp", None, channels),
        P(None, channels),
        P(None, channels),
        P(None, channels),
        P(channels),
        P(channels, None),
        P(None, None, channels),
        P(None, channels),
        P(channels),
        P(None, channels),
        P(channels),
        P(channels, None),
        P("expert", ("dp", "tensor"), None),
        P("expert", ("dp", "tensor"), None),
        P("expert", ("dp", "tensor"), None),
        P(None, rows, None),
        P(None, rows, None),
    )
    return jax.shard_map(
        shards,
        mesh=mesh,
        in_specs=placed,
        out_specs=(P(None, rows, None), P("dp", None, channels), P("dp", None, channels)),
        check_vma=False,
    )
```

```python
import functools

import jax
import jax.numpy as jnp
from jax import lax
from jax.experimental import pallas as pl
from jax.experimental.pallas import tpu as pltpu
from jax.sharding import PartitionSpec as P

MESH = pl.DeviceIdType.MESH
F32 = jnp.float32
BF16 = jnp.bfloat16
MIB = 2**20


def place():
    z, e, x = lax.axis_index("dp"), lax.axis_index("expert"), lax.axis_index("tensor")
    return z, lax.div(e, 2), lax.rem(e, 2), x


def remote(src, dst, sems, at, device):
    return pltpu.make_async_remote_copy(
        src_ref=src,
        dst_ref=dst,
        send_sem=sems[0].at[at],
        recv_sem=sems[1].at[at],
        device_id=device,
        device_id_type=MESH,
    )


def greet(devices):
    barrier = pltpu.get_barrier_semaphore()
    for device in devices:
        pl.semaphore_signal(barrier, inc=1, device_id=device, device_id_type=MESH)
    pl.semaphore_wait(barrier, len(devices))


def silu(v):
    return v / (1.0 + jnp.exp(-v))


PIECES = 4
SMALL = 7


def mixer_in_kernel(
    rows_hbm, inner_hbm, gate_hbm, *refs
):
    small_hbm, refs = refs[:SMALL], refs[SMALL:]
    conv_out, act_out, gate_out, size_out, state_out = refs[:5]
    small, refs = refs[5 : 5 + SMALL], refs[5 + SMALL :]
    (
    rows, inner, gate, local, part, got, both, recv, out, one, other, send_a, recv_a, send_b, recv_b
    ) = refs
    z, y, c, x = place()
    me = y * 4 + x
    width = 4096 // PIECES
    cuts = [pl.ds(k * width, width) for k in range(PIECES)]
    pairs = [p for k in cuts for p in ((rows_hbm.at[:, k], rows.at[:, k]), (inner_hbm.at[k], inner.at[k]))]
    pairs.extend(zip(small_hbm, small))
    pairs.extend((gate_hbm.at[k], gate.at[k]) for k in cuts)
    loads = [pltpu.make_async_copy(a, b, local.at[i]) for i, (a, b) in enumerate(pairs)]
    for load in loads:
        load.start()
    conv_state, conv_weight, conv_bias, delta_down, state_proj, delta_up, delta_bias = small
    small_loads, gate_loads = loads[2 * PIECES : 2 * PIECES + SMALL], loads[2 * PIECES + SMALL :]

    def chip(p):
        return (z, lax.div(p, 4) * 2 + c, lax.rem(p, 4))

    sibling = (z, y * 2 + 1 - c, x)
    barrier = pltpu.get_barrier_semaphore()
    pl.semaphore_signal(barrier, inc=1, device_id=sibling, device_id_type=MESH)

    def signal(i, carry):
        pl.semaphore_signal(
            barrier, inc=1, device_id=chip(lax.rem(me + i, 16)), device_id_type=MESH
        )
        return carry

    lax.fori_loop(1, 16, signal, 0)

    squares = jnp.zeros((256, 1), F32)
    conv_in = jnp.zeros((256, 128), F32)
    for k in range(PIECES):
        loads[2 * k].wait()
        loads[2 * k + 1].wait()
        piece = rows[:, k * width : (k + 1) * width]
        conv_in = conv_in + jnp.dot(
            piece, inner[k * width : (k + 1) * width], preferred_element_type=F32
        )
        wide = piece.astype(F32)
        squares = squares + jnp.sum(wide * wide, axis=1, keepdims=True)
    scale = lax.rsqrt(squares * (1.0 / 4096) + 1e-06)
    for load in small_loads:
        load.wait()
    conv_in = (conv_in * scale).astype(BF16)
    conv_out[0] = conv_state[2]
    conv_out[1] = conv_in[:128]
    conv_out[2] = conv_in[128:]
    conv_in = conv_in.astype(F32)
    window = [conv_state[k].astype(F32) for k in range(3)] + [conv_in[:128], conv_in[128:]]
    acts = []
    for s in range(2):
        total = conv_bias[...]
        for k in range(4):
            total = total + window[s + k] * conv_weight[k : k + 1]
        acts.append(silu(total))
    activated = jnp.concatenate(acts, axis=0).astype(BF16)
    act_out[...] = activated
    delta = jnp.dot(activated, delta_down[...], preferred_element_type=F32)
    state = lax.dot_general(
        activated, state_proj[...], (((1,), (1,)), ((), ())), preferred_element_type=F32
    )
    state = jnp.concatenate([state, jnp.zeros((256, 224), F32)], axis=1)
    blocks = jnp.concatenate([delta.reshape(32, 8, 256), state.reshape(32, 8, 256)], axis=1)
    part[...] = blocks.astype(BF16).reshape(2, 16, 16, 256)

    pl.semaphore_wait(barrier, 16)
    swap = remote(part.at[1 - c], got, (one, other), 0, sibling)
    swap.start()
    swap.wait()
    both[...] = (part[c].astype(F32) + got[...].astype(F32)).astype(BF16)

    def first(i):
        p = lax.rem(me + i, 16)
        return remote(both.at[p], recv.at[i - 1], (send_a, recv_a), i - 1, chip(p))

    def start_first(i, carry):
        first(i).start()
        return carry

    lax.fori_loop(1, 16, start_first, 0)

    gated = jnp.zeros((256, 128), F32)
    for k in range(PIECES):
        gate_loads[k].wait()
        gated = gated + jnp.dot(
            rows[:, k * width : (k + 1) * width],
            gate[k * width : (k + 1) * width],
            preferred_element_type=F32,
        )
    gate_out[...] = silu(gated * scale)

    def add(i, total):
        first(i).wait()
        return total + recv[i - 1].astype(F32)

    total = lax.fori_loop(1, 16, add, both[me].astype(F32))
    low, state = total[:8], total[8:]
    normed = low * lax.rsqrt(jnp.mean(low * low, axis=-1, keepdims=True) + 1e-06)
    high = state.astype(BF16).astype(F32)
    rest = state - high
    split = jnp.concatenate([high[:, :32], rest[:, :32], state[:, 64:]], axis=1)
    out[c, me] = jnp.concatenate([normed, split], axis=0).astype(BF16)

    def second(i):
        return remote(
            out.at[c, me], out.at[c, me], (send_b, recv_b), i - 1, chip(lax.rem(me + i, 16))
        )

    def second_from(i):
        p = lax.rem(me + 16 - i, 16)
        return remote(out.at[c, p], out.at[c, p], (send_b, recv_b), i - 1, chip(p))

    def start_second(i, carry):
        second(i).start()
        return carry

    lax.fori_loop(1, 16, start_second, 0)

    def wait_second(i, carry):
        second(i).wait_send()
        second_from(i).wait_recv()
        return carry

    lax.fori_loop(1, 16, wait_second, 0)
    swap = remote(out.at[c], out.at[c], (one, other), 1, sibling)
    swap.start()
    swap.wait_send()
    remote(out.at[1 - c], out.at[1 - c], (one, other), 1, sibling).wait_recv()
    summed = out[...].reshape(32, 16, 256).astype(F32)
    normed = summed[:, :8].reshape(256, 256).astype(BF16)
    value = jnp.dot(normed, delta_up[...], preferred_element_type=F32) + delta_bias[...]
    size_out[...] = jnp.maximum(value, 0.0) + jnp.log1p(jnp.exp(-jnp.abs(value)))
    state = summed[:, 8:].reshape(256, 256)
    state_out[...] = state[:, :64].astype(BF16)


def mixer_in(rows, inner, gate, *rest):
    vmem = pl.BlockSpec(memory_space=pltpu.VMEM)
    hbm = pl.BlockSpec(memory_space=pl.ANY)
    return pl.pallas_call(
        mixer_in_kernel,
        out_shape=(
            jax.ShapeDtypeStruct((3, 128, 128), BF16),
            jax.ShapeDtypeStruct((256, 128), BF16),
            jax.ShapeDtypeStruct((256, 128), F32),
            jax.ShapeDtypeStruct((256, 128), F32),
            jax.ShapeDtypeStruct((256, 64), BF16),
        ),
        in_specs=[hbm] * (3 + len(rest)),
        out_specs=(vmem,) * 5,
        scratch_shapes=[
            *(pltpu.VMEM(v.shape, v.dtype) for v in rest),
            pltpu.VMEM((256, 4096), BF16),
            pltpu.VMEM((4096, 128), BF16),
            pltpu.VMEM((4096, 128), BF16),
            pltpu.SemaphoreType.DMA((3 * PIECES + SMALL,)),
            pltpu.VMEM((2, 16, 16, 256), BF16),
            pltpu.VMEM((16, 16, 256), BF16),
            pltpu.VMEM((16, 16, 256), BF16),
            pltpu.VMEM((15, 16, 256), BF16),
            pltpu.VMEM((2, 16, 16, 256), BF16),
            pltpu.SemaphoreType.DMA((2,)),
            pltpu.SemaphoreType.DMA((2,)),
            pltpu.SemaphoreType.DMA((15,)),
            pltpu.SemaphoreType.DMA((15,)),
            pltpu.SemaphoreType.DMA((15,)),
            pltpu.SemaphoreType.DMA((15,)),
        ],
        compiler_params=pltpu.CompilerParams(
            collective_id=0, has_side_effects=True, vmem_limit_bytes=56 * MIB
        ),
        name="mixer_in",
    )(rows, inner, gate, *rest)


BLOCK = 64


def recurrence_kernel(size, act, gate, state_in, decay_log, skip, conv, before, gated, after, conv_out):
    rates = jnp.exp(decay_log[...])[None]
    held = before[...]
    conv_out[...] = conv[...]
    long = BLOCK * 16
    row, col = (lax.broadcasted_iota(jnp.int32, (long, BLOCK), d) for d in range(2))
    copy = jnp.where(row // 16 == col, 1.0, 0.0).astype(BF16)
    row, col = (lax.broadcasted_iota(jnp.int32, (long, 64), d) for d in range(2))
    masks = [jnp.where(col % 32 == k * 16 + row % 16, 1.0, 0.0) for k in range(2)]
    ones = jnp.ones((64, 128), BF16)
    for s in range(2):
        spread = jnp.dot(copy, state_in[s], preferred_element_type=F32)
        b_in, c_out = (
            jnp.dot((spread * m).astype(BF16), ones, preferred_element_type=F32).reshape(
                BLOCK, 16, 128
            )
            for m in masks
        )
        step = size[s]
        x = act[s].astype(F32)
        held = (
            jnp.exp(-step[:, None, :] * rates) * held + (step * x)[:, None, :] * b_in
        )
        readout = jnp.sum(held * c_out, axis=1)
        gated[s] = ((readout + skip[...] * x) * gate[s]).astype(BF16)
    after[...] = held


def recurrence(size, act, gate, state_in, decay_log, skip, conv, before):
    rows = pl.BlockSpec((2, BLOCK, 128), lambda i: (0, i, 0))
    state = pl.BlockSpec((BLOCK, 16, 128), lambda i: (i, 0, 0))
    return pl.pallas_call(
        recurrence_kernel,
        grid=(128 // BLOCK,),
        out_shape=(
            jax.ShapeDtypeStruct((2, 128, 128), BF16),
            jax.ShapeDtypeStruct((128, 16, 128), F32),
            jax.ShapeDtypeStruct((3, 128, 128), BF16),
        ),
        in_specs=[
            rows,
            rows,
            rows,
            pl.BlockSpec((2, BLOCK, 64), lambda i: (0, i, 0)),
            pl.BlockSpec((16, 128), lambda i: (0, 0)),
            pl.BlockSpec((1, 128), lambda i: (0, 0)),
            pl.BlockSpec((3, BLOCK, 128), lambda i: (0, i, 0)),
            state,
        ],
        out_specs=(rows, state, pl.BlockSpec((3, BLOCK, 128), lambda i: (0, i, 0))),
        compiler_params=pltpu.CompilerParams(vmem_limit_bytes=60 * MIB),
        name="recurrence",
    )(size, act, gate, state_in, decay_log, skip, conv, before)


def tables(ids, route, core):
    row, col = (lax.broadcasted_iota(jnp.int32, (8, 4), d) for d in range(2))
    own = row % 4 == col
    ids, route = (
        [jnp.sum(jnp.where(own, v[j : j + 1], 0), axis=1, keepdims=True) for j in range(2)]
        for v in (ids, route)
    )
    lane = lax.broadcasted_iota(jnp.int32, (8, 128), 1)
    named = [lane == ids[j] for j in range(2)]
    hit = (named[0] | named[1]).astype(F32)
    row, col = (lax.broadcasted_iota(jnp.int32, (8, 8), d) for d in range(2))
    earlier = ((col < row) & (col // 4 == row // 4)).astype(F32)
    count = jnp.dot(earlier, hit, preferred_element_type=F32)
    here = lax.broadcasted_iota(jnp.int32, (8, 1), 0) // 4 == core
    at = lax.broadcasted_iota(jnp.int32, (64, 128), 1)
    pick, mix = None, None
    for j in range(2):
        slot = jnp.sum(jnp.where(named[j], count, 0.0), axis=1, keepdims=True).astype(jnp.int32)
        target = jnp.where(here, ids[j] * 16 + slot, -64)
        mask = at == jnp.concatenate([target + 2 * k for k in range(8)], axis=0)
        weight = jnp.concatenate([route[j]] * 8, axis=0)
        one = jnp.where(mask, 1.0, 0.0)
        pick = one if j == 0 else pick + one
        mix = one * weight if j == 0 else mix + one * weight
    return pick.astype(BF16), mix


def swap_fields():
    row, col = (lax.broadcasted_iota(jnp.int32, (128, 128), d) for d in range(2))
    swapped = (row // 2 % 8) * 16 + (row // 16) * 2 + row % 2
    return jnp.where(col == swapped, 1.0, 0.0).astype(BF16)


GATHER = 22
REDUCE = 14


def expert_kernel(
    gated_hbm, weight_hbm, ids_hbm, route_hbm, layer_hbm, gate_hbm, up_hbm, down_hbm,
    out,
    gated, weight, ids, route, own, left, first, mine, got0, sums, got1, mid, got2, last, got3, residual,
    gate, up, down, message, arrived, rows, act, part, got_hop, got_full, quad, got_quad,
    reply, returned, local, ss, rs, mss, mrs,
):
    z, y, c, x = place()
    e = y * 2 + c
    sems = (ss, rs)
    mixer_sems = (mss, mrs)
    def dev_e(d):
        return (z, lax.rem(e + d, 8), x)

    def dev_x(d):
        return (z, e, lax.rem(x + d, 4))

    def dev_y(d):
        return (z, lax.rem(y + d, 4) * 2 + c, x)

    def dev_z(d):
        return (lax.rem(z + d, 4), e, x)

    sibling = (z, y * 2 + 1 - c, x)
    friends = [dev_e(d) for d in range(1, 8)] + [f(d) for f in (dev_x, dev_z) for d in (1, 2, 3)]
    barrier = pltpu.get_barrier_semaphore()
    for friend in friends:
        pl.semaphore_signal(barrier, inc=1, device_id=friend, device_id_type=MESH)

    early = [pltpu.make_async_copy(gated_hbm, gated, local.at[4])]
    for i in range(2):
        cols = pl.ds(pl.multiple_of(((1 - c) if i == 0 else c) * 2048, 2048), 2048)
        early.append(
            pltpu.make_async_copy(weight_hbm.at[:, cols], weight.at[:, cols], local.at[5 + i])
        )
    early.append(pltpu.make_async_copy(ids_hbm, ids, local.at[7]))
    early.append(pltpu.make_async_copy(route_hbm, route, local.at[8]))
    for load in early:
        load.start()
    chip_rows = pltpu.make_async_copy(
        layer_hbm.at[:, pl.ds(pl.multiple_of(y * 32, 32), 32)], own, local.at[3]
    )
    chip_rows.start()

    MIXER = 15
    other = 1 - c

    def product(s, half, q):
        cols = pl.ds(pl.multiple_of(half * 2048 + q * 1024, 1024), 1024)
        return jnp.dot(left[s], weight[:, cols], preferred_element_type=F32)

    def mixer_swap(s):
        copies = []
        for q in range(2):
            copy = remote(first.at[s, q], got0.at[s, q], mixer_sems, s * MIXER + q, sibling)
            copy.start()
            copies.append(copy)
        return copies

    def mixer_first(s, swaps):
        copies = []
        for q in range(2):
            swaps[q].wait()
            both = (mine[s, q] + got0[s, q].astype(F32)).reshape(4, 4, 8, 1024)
            both = jnp.concatenate([both[..., :512], both[..., 512:]], axis=2).astype(BF16)
            if q == 0:
                for at in range(4):
                    for to in range(4):
                        sums[s, q, to, at] = both[at, to]
            else:
                sums[s, q] = both
            dev, at = (dev_x, x) if q == 0 else (dev_y, y)
            for d in (1, 2, 3):
                copy = remote(
                    sums.at[s, q, lax.rem(at + d, 4)],
                    got1.at[s, q, d - 1],
                    mixer_sems,
                    s * MIXER + 2 + q * 3 + d - 1,
                    dev(d),
                )
                copy.start()
                copies.append(copy)
        return copies

    def mixer_second(s, ones):
        copies = []
        for q in range(2):
            for copy in ones[q * 3 : q * 3 + 3]:
                copy.wait()
            total = sums[s, q, x if q == 0 else y].astype(F32)
            for d in range(3):
                total = total + got1[s, q, d].astype(F32)
            mid[s, q] = total.astype(BF16)
            dev, at = (dev_y, y) if q == 0 else (dev_x, x)
            for d in (1, 2, 3):
                copy = remote(
                    mid.at[s, q, lax.rem(at + d, 4)],
                    got2.at[s, q, d - 1],
                    mixer_sems,
                    s * MIXER + 8 + q * 3 + d - 1,
                    dev(d),
                )
                copy.start()
                copies.append(copy)
        return copies

    def mixer_third(s, twos):
        for q in range(2):
            for copy in twos[q * 3 : q * 3 + 3]:
                copy.wait()
            total = mid[s, q, y if q == 0 else x].astype(F32)
            for d in range(3):
                total = total + got2[s, q, d].astype(F32)
            last[s, q] = total
        copy = remote(last.at[s], got3.at[s], mixer_sems, s * MIXER + 14, sibling)
        copy.start()
        return copy

    picks, mixes, helpers, sends = [], [], [], {}

    def rows_out(s, copy):
        if s == 0:
            chip_rows.wait()
        for half, source in ((c, last), (other, got3)):
            if source is got3:
                copy.wait()
            for q in range(2):
                for k in range(2):
                    cols = pl.ds(pl.multiple_of(half * 2048 + q * 1024 + k * 512, 512), 512)
                    step_rows = jnp.dot(helpers[1], own[s, :, cols], preferred_element_type=F32)
                    residual[s, :, cols] = source[s, q, k * 8 : k * 8 + 8] + step_rows[:8]
        value = residual[s]
        normed = value * lax.rsqrt(jnp.mean(value * value, axis=-1, keepdims=True) + 1e-06)
        stacked = jnp.concatenate([normed[:, k * 512 : (k + 1) * 512] for k in range(8)], axis=0)
        spread_rows = lax.dot_general(
            picks[s], stacked.astype(BF16), (((0,), (0,)), ((), ())), preferred_element_type=F32
        )
        message[s] = spread_rows.astype(BF16).reshape(8, 16, 512)
        for d in range(1, 8):
            copy = remote(
                message.at[s, lax.rem(e + d, 8)],
                arrived.at[s, e],
                sems,
                s * 7 + d - 1,
                dev_e(d),
            )
            copy.start()
            sends[s, d] = copy
        arrived[s, e] = message[s, e]

    base = 14
    halves = (slice(0, 2048), slice(2048, 4096))

    def first_gather(s):
        for d in range(1, 8):
            sends[s, d].wait()
        ordered = jnp.dot(
            helpers[0], arrived[s].reshape(128, 512), preferred_element_type=F32
        ).astype(BF16)
        for k in range(8):
            h, at = divmod(k, 4)
            rows[s, h, z, x, :, at * 512 : (at + 1) * 512] = ordered[k * 16 : (k + 1) * 16]
        copies = []
        for h in range(2):
            for d in (1, 2, 3):
                copy = remote(
                    rows.at[s, h, z, x],
                    rows.at[s, h, z, x],
                    sems,
                    base + s * GATHER + h * 3 + d - 1,
                    (dev_x if h == 0 else dev_z)(d),
                )
                copy.start()
                copies.append(copy)
        return copies

    def band(s, h, q, at, half=None):
        along = pl.ds(0, 4) if half is None else pl.ds(2 * half, 2)
        every, cols = slice(None), pl.ds(q * 1024, 1024)
        at = (at, along) if h == 0 else (along, at)
        return rows.at[(s, h, *at, every, cols)]

    def second_gather(s, firsts):
        copies = {}
        for q in range(2):
            for h in range(2):
                if q == 0:
                    for copy in firsts[h * 3 : h * 3 + 3]:
                        copy.wait()
                dev, at = (dev_z, z) if h == 0 else (dev_x, x)
                for i, d in enumerate((1, 3)):
                    mine_ = band(s, h, q, at)
                    n = base + s * GATHER + 6 + q * 8 + h * 4 + i
                    copy = remote(mine_, mine_, sems, n, dev(d))
                    copy.start()
                    copies[q, h, i] = copy
        return copies

    def third_gather(s, q, seconds):
        copies = []
        for h in range(2):
            dev, at = (dev_z, z) if h == 0 else (dev_x, x)
            for i, d in enumerate((1, 3)):
                seconds[q, h, i].wait()
                piece = band(s, h, q, lax.rem(at + 4 - d, 4), i)
                n = base + s * GATHER + 6 + q * 8 + h * 4 + 2 + i
                copy = remote(piece, piece, sems, n, dev(d))
                copy.start()
                copies.append(copy)
        return copies

    def compute(s, t):
        at = slice(t * 256, (t + 1) * 256)
        g = jnp.zeros((256, 256), F32)
        u = jnp.zeros((256, 256), F32)
        for h in range(2):
            piece = rows[s, h].reshape(256, 2048)
            nt = (((1,), (1,)), ((), ()))
            g = g + lax.dot_general(piece, gate[at, halves[h]], nt, preferred_element_type=F32)
            u = u + lax.dot_general(piece, up[at, halves[h]], nt, preferred_element_type=F32)
        act[:, at] = (silu(g) * u).astype(BF16)

    def project(s, q):
        for h in range(2):
            from_ = slice(h * 2048 + q * 1024, h * 2048 + (q + 1) * 1024)
            value = jnp.dot(act[...], down[:, from_], preferred_element_type=F32)
            part[s, h, q] = value.astype(BF16).reshape(4, 4, 16, 1024)

    base2 = base + 2 * GATHER

    def pband(s, h, q, at, half=None):
        along = pl.ds(0, 4) if half is None else pl.ds(2 * half, 2)
        return part.at[s, h, q, at, along] if h == 0 else part.at[s, h, q, along, at]

    def first_reduce(s, q):
        copies = []
        for h in range(2):
            dev, at = (dev_z, z) if h == 0 else (dev_x, x)
            far = lax.rem(at + 2, 4)
            for i, d in enumerate((1, 3)):
                copy = remote(
                    pband(s, h, q, far, i),
                    got_hop.at[s, h, q, i],
                    sems,
                    base2 + (s * 2 + q) * REDUCE + h * 4 + i,
                    dev(d),
                )
                copy.start()
                copies.append(copy)
        return copies

    def second_reduce(s, q, firsts):
        copies = []
        for h in range(2):
            dev, at = (dev_z, z) if h == 0 else (dev_x, x)
            for i, d in enumerate((1, 3)):
                firsts[h * 2 + i].wait()
                to = lax.rem(at + d, 4)
                for j in range(2):
                    k = (to, 2 * i + j) if h == 0 else (2 * i + j, to)
                    value = part[s, h, q, k[0], k[1]].astype(F32)
                    part[s, h, q, k[0], k[1]] = (
                        value + got_hop[s, h, q, i, j].astype(F32)
                    ).astype(BF16)
                copy = remote(
                    pband(s, h, q, to),
                    got_full.at[s, h, q, i],
                    sems,
                    base2 + (s * 2 + q) * REDUCE + h * 4 + 2 + i,
                    dev(d),
                )
                copy.start()
                copies.append(copy)
        return copies

    def third_reduce(s, q, seconds):
        copies = []
        for h in range(2):
            for i in range(2):
                seconds[h * 2 + i].wait()
            for j in range(4):
                kept = part[s, h, q, z, j] if h == 0 else part[s, h, q, j, x]
                total = kept.astype(F32)
                for i in range(2):
                    total = total + got_full[s, h, q, i, j].astype(F32)
                quad[s, h, q, j] = total.astype(BF16)
            dev, at = (dev_x, x) if h == 0 else (dev_z, z)
            for d in (1, 2, 3):
                copy = remote(
                    quad.at[s, h, q, lax.rem(at + d, 4)],
                    got_quad.at[s, h, q, d - 1],
                    sems,
                    base2 + (s * 2 + q) * REDUCE + 8 + h * 3 + d - 1,
                    dev(d),
                )
                copy.start()
                copies.append(copy)
        return copies

    base3 = base2 + 4 * REDUCE

    def send_back(s, thirds):
        pieces = []
        for h in range(2):
            for q in range(2):
                for copy in thirds[q][h * 3 : h * 3 + 3]:
                    copy.wait()
                at = x if h == 0 else z
                total = quad[s, h, q, at].astype(F32)
                for d in range(3):
                    total = total + got_quad[s, h, q, d].astype(F32)
                total = total.astype(BF16)
                pieces.extend((total[:, :512], total[:, 512:]))
        stack = jnp.concatenate(pieces, axis=0)
        value = jnp.dot(helpers[0], stack, preferred_element_type=F32).astype(BF16)
        reply[s] = value.reshape(8, 16, 512)
        copies = []
        for d in range(1, 8):
            copy = remote(
                reply.at[s, lax.rem(e + d, 8)],
                returned.at[s, e],
                sems,
                base3 + s * 7 + d - 1,
                dev_e(d),
            )
            copy.start()
            copies.append(copy)
        returned[s, e] = reply[s, e]
        return copies

    row, col = (lax.broadcasted_iota(jnp.int32, (128, 128), d) for d in range(2))
    moved = row // 32 * 32 + row // 4 % 2 * 16 + row // 8 % 4 * 4 + row % 4
    turn = jnp.where(col == moved, 1.0, 0.0).astype(BF16)
    swaps = []
    early[0].wait()
    early[1].wait()
    for s in range(2):
        left[s] = jnp.dot(turn, gated[s], preferred_element_type=F32).astype(BF16)
        for q in range(2):
            first[s, q] = product(s, other, q).astype(BF16)
        if s == 0:
            pl.semaphore_wait(barrier, len(friends))
        swaps.append(mixer_swap(s))
    early[2].wait()
    for s in range(2):
        for q in range(2):
            mine[s, q] = product(s, c, q)
    ones0 = mixer_first(0, swaps[0])
    ones1 = mixer_first(1, swaps[1])
    early[3].wait()
    early[4].wait()
    for s in range(2):
        pick, mix = tables(ids[s], route[s], c)
        picks.append(pick)
        mixes.append(mix)
    swap = swap_fields()
    row, col = (lax.broadcasted_iota(jnp.int32, (16, 32), d) for d in range(2))
    chosen = jnp.where(col == row // 4 * 16 + x * 4 + row % 4, 1.0, 0.0).astype(BF16)
    helpers.extend((swap, chosen))
    loads = []
    for i, (a, b) in enumerate(((gate_hbm, gate), (up_hbm, up), (down_hbm, down))):
        load = pltpu.make_async_copy(a.at[0], b, local.at[i])
        load.start()
        loads.append(load)
    twos0 = mixer_second(0, ones0)
    twos1 = mixer_second(1, ones1)
    last0 = mixer_third(0, twos0)
    rows_out(0, last0)
    last1 = mixer_third(1, twos1)
    first0 = first_gather(0)
    rows_out(1, last1)
    second0 = second_gather(0, first0)
    first1 = first_gather(1)
    third00 = third_gather(0, 0, second0)
    third01 = third_gather(0, 1, second0)
    second1 = second_gather(1, first1)
    for copy in third00 + third01:
        copy.wait()
    for load in loads[:2]:
        load.wait()
    compute(0, 0)
    third10 = third_gather(1, 0, second1)
    compute(0, 1)
    loads[2].wait()
    project(0, 0)
    hop00 = first_reduce(0, 0)
    third11 = third_gather(1, 1, second1)
    project(0, 1)
    hop01 = first_reduce(0, 1)
    full00 = second_reduce(0, 0, hop00)
    full01 = second_reduce(0, 1, hop01)
    for copy in third10 + third11:
        copy.wait()
    compute(1, 0)
    compute(1, 1)
    project(1, 0)
    hop10 = first_reduce(1, 0)
    quad00 = third_reduce(0, 0, full00)
    project(1, 1)
    hop11 = first_reduce(1, 1)
    quad01 = third_reduce(0, 1, full01)
    full10 = second_reduce(1, 0, hop10)
    full11 = second_reduce(1, 1, hop11)
    back0 = send_back(0, (quad00, quad01))
    quad10 = third_reduce(1, 0, full10)
    quad11 = third_reduce(1, 1, full11)
    back1 = send_back(1, (quad10, quad11))
    for s in range(2):
        for copy in (back0, back1)[s]:
            copy.wait()
        replies = returned[s].reshape(128, 512)
        high = mixes[s].astype(BF16)
        low = (mixes[s] - high.astype(F32)).astype(BF16)
        value = jnp.dot(high, replies, preferred_element_type=F32)
        value = value + jnp.dot(low, replies, preferred_element_type=F32)
        for k in range(8):
            cols = slice(k * 512, (k + 1) * 512)
            total = residual[s, :, cols] + value[k * 8 : (k + 1) * 8]
            out[s, :, cols] = jnp.where(c == 0, total[:4], total[4:])


def expert_layer(gated, weight, ids, route, layer_in, gate, up, down):
    vmem = pl.BlockSpec(memory_space=pltpu.VMEM)
    hbm = pl.BlockSpec(memory_space=pl.ANY)
    count = 14 + 2 * GATHER + 4 * REDUCE + 14
    return pl.pallas_call(
        expert_kernel,
        out_shape=jax.ShapeDtypeStruct((2, 4, 4096), F32),
        in_specs=[hbm] * 8,
        out_specs=vmem,
        scratch_shapes=[
            pltpu.VMEM((2, 128, 128), BF16),
            pltpu.VMEM((128, 4096), BF16),
            pltpu.VMEM((2, 2, 4), jnp.int32),
            pltpu.VMEM((2, 2, 4), F32),
            pltpu.VMEM((2, 32, 4096), BF16),
            pltpu.VMEM((2, 128, 128), BF16),
            pltpu.VMEM((2, 2, 128, 1024), BF16),
            pltpu.VMEM((2, 2, 128, 1024), F32),
            pltpu.VMEM((2, 2, 128, 1024), BF16),
            pltpu.VMEM((2, 2, 4, 4, 16, 512), BF16),
            pltpu.VMEM((2, 2, 3, 4, 16, 512), BF16),
            pltpu.VMEM((2, 2, 4, 16, 512), BF16),
            pltpu.VMEM((2, 2, 3, 16, 512), BF16),
            pltpu.VMEM((2, 2, 16, 512), F32),
            pltpu.VMEM((2, 2, 16, 512), F32),
            pltpu.VMEM((2, 8, 4096), F32),
            pltpu.VMEM((512, 4096), BF16),
            pltpu.VMEM((512, 4096), BF16),
            pltpu.VMEM((512, 4096), BF16),
            pltpu.VMEM((2, 8, 16, 512), BF16),
            pltpu.VMEM((2, 8, 16, 512), BF16),
            pltpu.VMEM((2, 2, 4, 4, 16, 2048), BF16),
            pltpu.VMEM((256, 512), BF16),
            pltpu.VMEM((2, 2, 2, 4, 4, 16, 1024), BF16),
            pltpu.VMEM((2, 2, 2, 2, 2, 16, 1024), BF16),
            pltpu.VMEM((2, 2, 2, 2, 4, 16, 1024), BF16),
            pltpu.VMEM((2, 2, 2, 4, 16, 1024), BF16),
            pltpu.VMEM((2, 2, 2, 3, 16, 1024), BF16),
            pltpu.VMEM((2, 8, 16, 512), BF16),
            pltpu.VMEM((2, 8, 16, 512), BF16),
            pltpu.SemaphoreType.DMA((9,)),
            pltpu.SemaphoreType.DMA((count,)),
            pltpu.SemaphoreType.DMA((count,)),
            pltpu.SemaphoreType.DMA((30,)),
            pltpu.SemaphoreType.DMA((30,)),
        ],
        compiler_params=pltpu.CompilerParams(
            collective_id=1, has_side_effects=True, vmem_limit_bytes=60 * MIB
        ),
        name="experts",
    )(gated, weight, ids, route, layer_in, gate, up, down)


def finish_kernel(value, out):
    out[...] = value[...].astype(BF16)


def finish(value):
    vmem = pl.BlockSpec(memory_space=pltpu.VMEM)
    return pl.pallas_call(
        finish_kernel,
        out_shape=jax.ShapeDtypeStruct(value.shape, BF16),
        in_specs=[vmem],
        out_specs=vmem,
        name="finish",
    )(value)


def shards(
    layer_in,
    conv_state,
    ssm_state,
    proj_inner,
    proj_gate,
    conv_weight,
    conv_bias,
    delta_down,
    state_proj,
    delta_up,
    delta_bias,
    decay_log,
    skip_gain,
    proj_out,
    expert_gate,
    expert_up,
    expert_down,
    expert_ids,
    route_weight,
):
    conv_final, activated, gate_branch, step_size, state_in = mixer_in(
        layer_in.reshape(256, 4096),
        proj_inner,
        proj_gate,
        jnp.transpose(conv_state, (1, 0, 2)),
        conv_weight,
        conv_bias[None],
        delta_down,
        state_proj.reshape(32, 128),
        delta_up,
        delta_bias[None],
    )
    gated, ssm_state, conv_final = recurrence(
        step_size.reshape(2, 128, 128),
        activated.reshape(2, 128, 128),
        gate_branch.reshape(2, 128, 128),
        state_in.reshape(2, 128, 64),
        decay_log,
        skip_gain[None],
        conv_final,
        ssm_state,
    )
    conv_final = jnp.transpose(conv_final, (1, 0, 2))
    layer_out = expert_layer(
        gated,
        proj_out,
        jnp.transpose(expert_ids, (0, 2, 1)),
        jnp.transpose(route_weight, (0, 2, 1)),
        layer_in,
        expert_gate,
        expert_up,
        expert_down,
    )
    return (finish(layer_out), conv_final, ssm_state)


def solution(mesh):
    channels = ("expert", "tensor")
    rows = ("dp", "expert", "tensor")
    placed = (
        P(None, "dp", None),
        P("dp", None, channels),
        P("dp", None, channels),
        P(None, channels),
        P(None, channels),
        P(None, channels),
        P(channels),
        P(channels, None),
        P(None, None, channels),
        P(None, channels),
        P(channels),
        P(None, channels),
        P(channels),
        P(channels, None),
        P("expert", ("dp", "tensor"), None),
        P("expert", ("dp", "tensor"), None),
        P("expert", ("dp", "tensor"), None),
        P(None, rows, None),
        P(None, rows, None),
    )
    return jax.shard_map(
        shards,
        mesh=mesh,
        in_specs=placed,
        out_specs=(P(None, rows, None), P("dp", None, channels), P("dp", None, channels)),
        check_vma=False,
    )
```

```python
import functools

import jax
import jax.numpy as jnp
from jax import lax
from jax.experimental import pallas as pl
from jax.experimental.pallas import tpu as pltpu
from jax.sharding import PartitionSpec as P

MESH = pl.DeviceIdType.MESH
F32 = jnp.float32
BF16 = jnp.bfloat16
MIB = 2**20


def place():
    z, e, x = lax.axis_index("dp"), lax.axis_index("expert"), lax.axis_index("tensor")
    return z, lax.div(e, 2), lax.rem(e, 2), x


def remote(src, dst, sems, at, device):
    return pltpu.make_async_remote_copy(
        src_ref=src,
        dst_ref=dst,
        send_sem=sems[0].at[at],
        recv_sem=sems[1].at[at],
        device_id=device,
        device_id_type=MESH,
    )


def greet(devices):
    barrier = pltpu.get_barrier_semaphore()
    for device in devices:
        pl.semaphore_signal(barrier, inc=1, device_id=device, device_id_type=MESH)
    pl.semaphore_wait(barrier, len(devices))


def silu(v):
    return v / (1.0 + jnp.exp(-v))


PIECES = 4
SMALL = 7


def mixer_in_kernel(
    rows_hbm, inner_hbm, gate_hbm, *refs
):
    small_hbm, refs = refs[:SMALL], refs[SMALL:]
    conv_out, act_out, gate_out, size_out, state_out = refs[:5]
    small, refs = refs[5 : 5 + SMALL], refs[5 + SMALL :]
    (
    rows, inner, gate, local, part, got, both, recv, out, one, other, send_a, recv_a, send_b, recv_b
    ) = refs
    z, y, c, x = place()
    me = y * 4 + x
    width = 4096 // PIECES
    cuts = [pl.ds(k * width, width) for k in range(PIECES)]
    pairs = [p for k in cuts for p in ((rows_hbm.at[:, k], rows.at[:, k]), (inner_hbm.at[k], inner.at[k]))]
    pairs.extend(zip(small_hbm, small))
    pairs.extend((gate_hbm.at[k], gate.at[k]) for k in cuts)
    loads = [pltpu.make_async_copy(a, b, local.at[i]) for i, (a, b) in enumerate(pairs)]
    for load in loads:
        load.start()
    conv_state, conv_weight, conv_bias, delta_down, state_proj, delta_up, delta_bias = small
    small_loads, gate_loads = loads[2 * PIECES : 2 * PIECES + SMALL], loads[2 * PIECES + SMALL :]

    def chip(p):
        return (z, lax.div(p, 4) * 2 + c, lax.rem(p, 4))

    sibling = (z, y * 2 + 1 - c, x)
    barrier = pltpu.get_barrier_semaphore()
    pl.semaphore_signal(barrier, inc=1, device_id=sibling, device_id_type=MESH)

    def signal(i, carry):
        pl.semaphore_signal(
            barrier, inc=1, device_id=chip(lax.rem(me + i, 16)), device_id_type=MESH
        )
        return carry

    lax.fori_loop(1, 16, signal, 0)

    squares = jnp.zeros((256, 1), F32)
    conv_in = jnp.zeros((256, 128), F32)
    for k in range(PIECES):
        loads[2 * k].wait()
        loads[2 * k + 1].wait()
        piece = rows[:, k * width : (k + 1) * width]
        conv_in = conv_in + jnp.dot(
            piece, inner[k * width : (k + 1) * width], preferred_element_type=F32
        )
        wide = piece.astype(F32)
        squares = squares + jnp.sum(wide * wide, axis=1, keepdims=True)
    scale = lax.rsqrt(squares * (1.0 / 4096) + 1e-06)
    for load in small_loads:
        load.wait()
    conv_in = (conv_in * scale).astype(BF16)
    conv_out[0] = conv_state[2]
    conv_out[1] = conv_in[:128]
    conv_out[2] = conv_in[128:]
    conv_in = conv_in.astype(F32)
    window = [conv_state[k].astype(F32) for k in range(3)] + [conv_in[:128], conv_in[128:]]
    acts = []
    for s in range(2):
        total = conv_bias[...]
        for k in range(4):
            total = total + window[s + k] * conv_weight[k : k + 1]
        acts.append(silu(total))
    activated = jnp.concatenate(acts, axis=0).astype(BF16)
    act_out[...] = activated
    delta = jnp.dot(activated, delta_down[...], preferred_element_type=F32)
    state = lax.dot_general(
        activated, state_proj[...], (((1,), (1,)), ((), ())), preferred_element_type=F32
    )
    state = jnp.concatenate([state, jnp.zeros((256, 224), F32)], axis=1)
    blocks = jnp.concatenate([delta.reshape(32, 8, 256), state.reshape(32, 8, 256)], axis=1)
    part[...] = blocks.astype(BF16).reshape(2, 16, 16, 256)

    pl.semaphore_wait(barrier, 16)
    swap = remote(part.at[1 - c], got, (one, other), 0, sibling)
    swap.start()
    swap.wait()
    both[...] = (part[c].astype(F32) + got[...].astype(F32)).astype(BF16)

    def first(i):
        p = lax.rem(me + i, 16)
        return remote(both.at[p], recv.at[i - 1], (send_a, recv_a), i - 1, chip(p))

    def start_first(i, carry):
        first(i).start()
        return carry

    lax.fori_loop(1, 16, start_first, 0)

    gated = jnp.zeros((256, 128), F32)
    for k in range(PIECES):
        gate_loads[k].wait()
        gated = gated + jnp.dot(
            rows[:, k * width : (k + 1) * width],
            gate[k * width : (k + 1) * width],
            preferred_element_type=F32,
        )
    gate_out[...] = silu(gated * scale)

    def add(i, total):
        first(i).wait()
        return total + recv[i - 1].astype(F32)

    total = lax.fori_loop(1, 16, add, both[me].astype(F32))
    low, state = total[:8], total[8:]
    normed = low * lax.rsqrt(jnp.mean(low * low, axis=-1, keepdims=True) + 1e-06)
    high = state.astype(BF16).astype(F32)
    rest = state - high
    split = jnp.concatenate([high[:, :32], rest[:, :32], state[:, 64:]], axis=1)
    out[c, me] = jnp.concatenate([normed, split], axis=0).astype(BF16)

    def second(i):
        return remote(
            out.at[c, me], out.at[c, me], (send_b, recv_b), i - 1, chip(lax.rem(me + i, 16))
        )

    def second_from(i):
        p = lax.rem(me + 16 - i, 16)
        return remote(out.at[c, p], out.at[c, p], (send_b, recv_b), i - 1, chip(p))

    def start_second(i, carry):
        second(i).start()
        return carry

    lax.fori_loop(1, 16, start_second, 0)

    def wait_second(i, carry):
        second(i).wait_send()
        second_from(i).wait_recv()
        return carry

    lax.fori_loop(1, 16, wait_second, 0)
    swap = remote(out.at[c], out.at[c], (one, other), 1, sibling)
    swap.start()
    swap.wait_send()
    remote(out.at[1 - c], out.at[1 - c], (one, other), 1, sibling).wait_recv()
    summed = out[...].reshape(32, 16, 256).astype(F32)
    normed = summed[:, :8].reshape(256, 256).astype(BF16)
    value = jnp.dot(normed, delta_up[...], preferred_element_type=F32) + delta_bias[...]
    size_out[...] = jnp.maximum(value, 0.0) + jnp.log1p(jnp.exp(-jnp.abs(value)))
    state = summed[:, 8:].reshape(256, 256)
    state_out[...] = state[:, :64].astype(BF16)


def mixer_in(rows, inner, gate, *rest):
    vmem = pl.BlockSpec(memory_space=pltpu.VMEM)
    hbm = pl.BlockSpec(memory_space=pl.ANY)
    return pl.pallas_call(
        mixer_in_kernel,
        out_shape=(
            jax.ShapeDtypeStruct((3, 128, 128), BF16),
            jax.ShapeDtypeStruct((256, 128), BF16),
            jax.ShapeDtypeStruct((256, 128), F32),
            jax.ShapeDtypeStruct((256, 128), F32),
            jax.ShapeDtypeStruct((256, 64), BF16),
        ),
        in_specs=[hbm] * (3 + len(rest)),
        out_specs=(vmem,) * 5,
        scratch_shapes=[
            *(pltpu.VMEM(v.shape, v.dtype) for v in rest),
            pltpu.VMEM((256, 4096), BF16),
            pltpu.VMEM((4096, 128), BF16),
            pltpu.VMEM((4096, 128), BF16),
            pltpu.SemaphoreType.DMA((3 * PIECES + SMALL,)),
            pltpu.VMEM((2, 16, 16, 256), BF16),
            pltpu.VMEM((16, 16, 256), BF16),
            pltpu.VMEM((16, 16, 256), BF16),
            pltpu.VMEM((15, 16, 256), BF16),
            pltpu.VMEM((2, 16, 16, 256), BF16),
            pltpu.SemaphoreType.DMA((2,)),
            pltpu.SemaphoreType.DMA((2,)),
            pltpu.SemaphoreType.DMA((15,)),
            pltpu.SemaphoreType.DMA((15,)),
            pltpu.SemaphoreType.DMA((15,)),
            pltpu.SemaphoreType.DMA((15,)),
        ],
        compiler_params=pltpu.CompilerParams(
            collective_id=0, has_side_effects=True, vmem_limit_bytes=56 * MIB
        ),
        name="mixer_in",
    )(rows, inner, gate, *rest)


BLOCK = 64


def recurrence_kernel(size, act, gate, state_in, decay_log, skip, conv, before, gated, after, conv_out):
    rates = jnp.exp(decay_log[...])[None]
    held = before[...]
    conv_out[...] = conv[...]
    long = BLOCK * 16
    row, col = (lax.broadcasted_iota(jnp.int32, (long, BLOCK), d) for d in range(2))
    copy = jnp.where(row // 16 == col, 1.0, 0.0).astype(BF16)
    row, col = (lax.broadcasted_iota(jnp.int32, (long, 64), d) for d in range(2))
    masks = [jnp.where(col % 32 == k * 16 + row % 16, 1.0, 0.0) for k in range(2)]
    ones = jnp.ones((64, 128), BF16)
    for s in range(2):
        spread = jnp.dot(copy, state_in[s], preferred_element_type=F32)
        b_in, c_out = (
            jnp.dot((spread * m).astype(BF16), ones, preferred_element_type=F32).reshape(
                BLOCK, 16, 128
            )
            for m in masks
        )
        step = size[s]
        x = act[s].astype(F32)
        held = (
            jnp.exp(-step[:, None, :] * rates) * held + (step * x)[:, None, :] * b_in
        )
        readout = jnp.sum(held * c_out, axis=1)
        gated[s] = ((readout + skip[...] * x) * gate[s]).astype(BF16)
    after[...] = held


def recurrence(size, act, gate, state_in, decay_log, skip, conv, before):
    rows = pl.BlockSpec((2, BLOCK, 128), lambda i: (0, i, 0))
    state = pl.BlockSpec((BLOCK, 16, 128), lambda i: (i, 0, 0))
    return pl.pallas_call(
        recurrence_kernel,
        grid=(128 // BLOCK,),
        out_shape=(
            jax.ShapeDtypeStruct((2, 128, 128), BF16),
            jax.ShapeDtypeStruct((128, 16, 128), F32),
            jax.ShapeDtypeStruct((3, 128, 128), BF16),
        ),
        in_specs=[
            rows,
            rows,
            rows,
            pl.BlockSpec((2, BLOCK, 64), lambda i: (0, i, 0)),
            pl.BlockSpec((16, 128), lambda i: (0, 0)),
            pl.BlockSpec((1, 128), lambda i: (0, 0)),
            pl.BlockSpec((3, BLOCK, 128), lambda i: (0, i, 0)),
            state,
        ],
        out_specs=(rows, state, pl.BlockSpec((3, BLOCK, 128), lambda i: (0, i, 0))),
        compiler_params=pltpu.CompilerParams(vmem_limit_bytes=60 * MIB),
        name="recurrence",
    )(size, act, gate, state_in, decay_log, skip, conv, before)


def tables(ids, route, core):
    row, col = (lax.broadcasted_iota(jnp.int32, (8, 4), d) for d in range(2))
    own = row % 4 == col
    ids, route = (
        [jnp.sum(jnp.where(own, v[j : j + 1], 0), axis=1, keepdims=True) for j in range(2)]
        for v in (ids, route)
    )
    lane = lax.broadcasted_iota(jnp.int32, (8, 128), 1)
    named = [lane == ids[j] for j in range(2)]
    hit = (named[0] | named[1]).astype(F32)
    row, col = (lax.broadcasted_iota(jnp.int32, (8, 8), d) for d in range(2))
    earlier = ((col < row) & (col // 4 == row // 4)).astype(F32)
    count = jnp.dot(earlier, hit, preferred_element_type=F32)
    here = lax.broadcasted_iota(jnp.int32, (8, 1), 0) // 4 == core
    at = lax.broadcasted_iota(jnp.int32, (64, 128), 1)
    pick, mix = None, None
    for j in range(2):
        slot = jnp.sum(jnp.where(named[j], count, 0.0), axis=1, keepdims=True).astype(jnp.int32)
        target = jnp.where(here, ids[j] * 16 + slot, -64)
        mask = at == jnp.concatenate([target + 2 * k for k in range(8)], axis=0)
        weight = jnp.concatenate([route[j]] * 8, axis=0)
        one = jnp.where(mask, 1.0, 0.0)
        pick = one if j == 0 else pick + one
        mix = one * weight if j == 0 else mix + one * weight
    return pick.astype(BF16), mix


def swap_fields():
    row, col = (lax.broadcasted_iota(jnp.int32, (128, 128), d) for d in range(2))
    swapped = (row // 2 % 8) * 16 + (row // 16) * 2 + row % 2
    return jnp.where(col == swapped, 1.0, 0.0).astype(BF16)


GATHER = 22
REDUCE = 14


def expert_kernel(
    gated_hbm, weight_hbm, ids_hbm, route_hbm, layer_hbm, gate_hbm, up_hbm, down_hbm,
    out,
    gated, weight, ids, route, own, left, first, mine, got0, sums, got1, mid, got2, last, got3, residual,
    gate, up, down, message, arrived, rows, act, part, got_hop, got_full, quad, got_quad,
    reply, returned, local, ss, rs, mss, mrs,
):
    z, y, c, x = place()
    e = y * 2 + c
    sems = (ss, rs)
    mixer_sems = (mss, mrs)
    def dev_e(d):
        return (z, lax.rem(e + d, 8), x)

    def dev_x(d):
        return (z, e, lax.rem(x + d, 4))

    def dev_y(d):
        return (z, lax.rem(y + d, 4) * 2 + c, x)

    def dev_z(d):
        return (lax.rem(z + d, 4), e, x)

    sibling = (z, y * 2 + 1 - c, x)
    friends = [dev_e(d) for d in range(1, 8)] + [f(d) for f in (dev_x, dev_z) for d in (1, 2, 3)]
    barrier = pltpu.get_barrier_semaphore()
    for friend in friends:
        pl.semaphore_signal(barrier, inc=1, device_id=friend, device_id_type=MESH)

    early = [pltpu.make_async_copy(gated_hbm, gated, local.at[4])]
    for i in range(2):
        cols = pl.ds(pl.multiple_of(((1 - c) if i == 0 else c) * 2048, 2048), 2048)
        early.append(
            pltpu.make_async_copy(weight_hbm.at[:, cols], weight.at[:, cols], local.at[5 + i])
        )
    early.append(pltpu.make_async_copy(ids_hbm, ids, local.at[7]))
    early.append(pltpu.make_async_copy(route_hbm, route, local.at[8]))
    for load in early:
        load.start()
    chip_rows = pltpu.make_async_copy(
        layer_hbm.at[:, pl.ds(pl.multiple_of(y * 32, 32), 32)], own, local.at[3]
    )
    chip_rows.start()

    MIXER = 15
    other = 1 - c

    def product(s, half, q):
        cols = pl.ds(pl.multiple_of(half * 2048 + q * 1024, 1024), 1024)
        return jnp.dot(left[s], weight[:, cols], preferred_element_type=F32)

    def mixer_swap(s):
        copies = []
        for q in range(2):
            copy = remote(first.at[s, q], got0.at[s, q], mixer_sems, s * MIXER + q, sibling)
            copy.start()
            copies.append(copy)
        return copies

    def mixer_first(s, swaps):
        copies = []
        for q in range(2):
            swaps[q].wait()
            both = (mine[s, q] + got0[s, q].astype(F32)).reshape(4, 4, 8, 1024)
            both = jnp.concatenate([both[..., :512], both[..., 512:]], axis=2).astype(BF16)
            if q == 0:
                for at in range(4):
                    for to in range(4):
                        sums[s, q, to, at] = both[at, to]
            else:
                sums[s, q] = both
            dev, at = (dev_x, x) if q == 0 else (dev_y, y)
            for d in (1, 2, 3):
                copy = remote(
                    sums.at[s, q, lax.rem(at + d, 4)],
                    got1.at[s, q, d - 1],
                    mixer_sems,
                    s * MIXER + 2 + q * 3 + d - 1,
                    dev(d),
                )
                copy.start()
                copies.append(copy)
        return copies

    def mixer_second(s, ones):
        copies = []
        for q in range(2):
            for copy in ones[q * 3 : q * 3 + 3]:
                copy.wait()
            total = sums[s, q, x if q == 0 else y].astype(F32)
            for d in range(3):
                total = total + got1[s, q, d].astype(F32)
            mid[s, q] = total.astype(BF16)
            dev, at = (dev_y, y) if q == 0 else (dev_x, x)
            for d in (1, 2, 3):
                copy = remote(
                    mid.at[s, q, lax.rem(at + d, 4)],
                    got2.at[s, q, d - 1],
                    mixer_sems,
                    s * MIXER + 8 + q * 3 + d - 1,
                    dev(d),
                )
                copy.start()
                copies.append(copy)
        return copies

    def mixer_third(s, twos):
        for q in range(2):
            for copy in twos[q * 3 : q * 3 + 3]:
                copy.wait()
            total = mid[s, q, y if q == 0 else x].astype(F32)
            for d in range(3):
                total = total + got2[s, q, d].astype(F32)
            last[s, q] = total
        copy = remote(last.at[s], got3.at[s], mixer_sems, s * MIXER + 14, sibling)
        copy.start()
        return copy

    picks, mixes, helpers, sends = [], [], [], {}

    def rows_out(s, copy):
        if s == 0:
            chip_rows.wait()
        for half, source in ((c, last), (other, got3)):
            if source is got3:
                copy.wait()
            for q in range(2):
                for k in range(2):
                    cols = pl.ds(pl.multiple_of(half * 2048 + q * 1024 + k * 512, 512), 512)
                    step_rows = jnp.dot(helpers[1], own[s, :, cols], preferred_element_type=F32)
                    residual[s, :, cols] = source[s, q, k * 8 : k * 8 + 8] + step_rows[:8]
        value = residual[s]
        normed = value * lax.rsqrt(jnp.mean(value * value, axis=-1, keepdims=True) + 1e-06)
        stacked = jnp.concatenate([normed[:, k * 512 : (k + 1) * 512] for k in range(8)], axis=0)
        spread_rows = lax.dot_general(
            picks[s], stacked.astype(BF16), (((0,), (0,)), ((), ())), preferred_element_type=F32
        )
        message[s] = spread_rows.astype(BF16).reshape(8, 16, 512)
        for d in range(1, 8):
            copy = remote(
                message.at[s, lax.rem(e + d, 8)],
                arrived.at[s, e],
                sems,
                s * 7 + d - 1,
                dev_e(d),
            )
            copy.start()
            sends[s, d] = copy
        arrived[s, e] = message[s, e]

    base = 14
    halves = (slice(0, 2048), slice(2048, 4096))

    def first_gather(s):
        for d in range(1, 8):
            sends[s, d].wait()
        ordered = jnp.dot(
            helpers[0], arrived[s].reshape(128, 512), preferred_element_type=F32
        ).astype(BF16)
        for k in range(8):
            h, at = divmod(k, 4)
            rows[s, h, z, x, :, at * 512 : (at + 1) * 512] = ordered[k * 16 : (k + 1) * 16]
        copies = []
        for h in range(2):
            for d in (1, 2, 3):
                copy = remote(
                    rows.at[s, h, z, x],
                    rows.at[s, h, z, x],
                    sems,
                    base + s * GATHER + h * 3 + d - 1,
                    (dev_x if h == 0 else dev_z)(d),
                )
                copy.start()
                copies.append(copy)
        return copies

    def band(s, h, q, at, half=None):
        along = pl.ds(0, 4) if half is None else pl.ds(2 * half, 2)
        every, cols = slice(None), pl.ds(q * 1024, 1024)
        at = (at, along) if h == 0 else (along, at)
        return rows.at[(s, h, *at, every, cols)]

    def second_gather(s, firsts):
        copies = {}
        for q in range(2):
            for h in range(2):
                if q == 0:
                    for copy in firsts[h * 3 : h * 3 + 3]:
                        copy.wait()
                dev, at = (dev_z, z) if h == 0 else (dev_x, x)
                for i, d in enumerate((1, 3)):
                    mine_ = band(s, h, q, at)
                    n = base + s * GATHER + 6 + q * 8 + h * 4 + i
                    copy = remote(mine_, mine_, sems, n, dev(d))
                    copy.start()
                    copies[q, h, i] = copy
        return copies

    def third_gather(s, q, seconds):
        copies = []
        for h in range(2):
            dev, at = (dev_z, z) if h == 0 else (dev_x, x)
            for i, d in enumerate((1, 3)):
                seconds[q, h, i].wait()
                piece = band(s, h, q, lax.rem(at + 4 - d, 4), i)
                n = base + s * GATHER + 6 + q * 8 + h * 4 + 2 + i
                copy = remote(piece, piece, sems, n, dev(d))
                copy.start()
                copies.append(copy)
        return copies

    def compute(s, t):
        at = slice(t * 256, (t + 1) * 256)
        g = jnp.zeros((256, 256), F32)
        u = jnp.zeros((256, 256), F32)
        for h in range(2):
            piece = rows[s, h].reshape(256, 2048)
            nt = (((1,), (1,)), ((), ()))
            g = g + lax.dot_general(piece, gate[at, halves[h]], nt, preferred_element_type=F32)
            u = u + lax.dot_general(piece, up[at, halves[h]], nt, preferred_element_type=F32)
        act[:, at] = (silu(g) * u).astype(BF16)

    def project(s, q):
        for h in range(2):
            from_ = slice(h * 2048 + q * 1024, h * 2048 + (q + 1) * 1024)
            value = jnp.dot(act[...], down[:, from_], preferred_element_type=F32)
            part[s, h, q] = value.astype(BF16).reshape(4, 4, 16, 1024)

    base2 = base + 2 * GATHER

    def pband(s, h, q, at, half=None):
        along = pl.ds(0, 4) if half is None else pl.ds(2 * half, 2)
        return part.at[s, h, q, at, along] if h == 0 else part.at[s, h, q, along, at]

    def first_reduce(s, q):
        copies = []
        for h in range(2):
            dev, at = (dev_z, z) if h == 0 else (dev_x, x)
            far = lax.rem(at + 2, 4)
            for i, d in enumerate((1, 3)):
                copy = remote(
                    pband(s, h, q, far, i),
                    got_hop.at[s, h, q, i],
                    sems,
                    base2 + (s * 2 + q) * REDUCE + h * 4 + i,
                    dev(d),
                )
                copy.start()
                copies.append(copy)
        return copies

    def second_reduce(s, q, firsts):
        copies = []
        for h in range(2):
            dev, at = (dev_z, z) if h == 0 else (dev_x, x)
            for i, d in enumerate((1, 3)):
                firsts[h * 2 + i].wait()
                to = lax.rem(at + d, 4)
                for j in range(2):
                    k = (to, 2 * i + j) if h == 0 else (2 * i + j, to)
                    value = part[s, h, q, k[0], k[1]].astype(F32)
                    part[s, h, q, k[0], k[1]] = (
                        value + got_hop[s, h, q, i, j].astype(F32)
                    ).astype(BF16)
                copy = remote(
                    pband(s, h, q, to),
                    got_full.at[s, h, q, i],
                    sems,
                    base2 + (s * 2 + q) * REDUCE + h * 4 + 2 + i,
                    dev(d),
                )
                copy.start()
                copies.append(copy)
        return copies

    def third_reduce(s, q, seconds):
        copies = []
        for h in range(2):
            for i in range(2):
                seconds[h * 2 + i].wait()
            for j in range(4):
                kept = part[s, h, q, z, j] if h == 0 else part[s, h, q, j, x]
                total = kept.astype(F32)
                for i in range(2):
                    total = total + got_full[s, h, q, i, j].astype(F32)
                quad[s, h, q, j] = total.astype(BF16)
            dev, at = (dev_x, x) if h == 0 else (dev_z, z)
            for d in (1, 2, 3):
                copy = remote(
                    quad.at[s, h, q, lax.rem(at + d, 4)],
                    got_quad.at[s, h, q, d - 1],
                    sems,
                    base2 + (s * 2 + q) * REDUCE + 8 + h * 3 + d - 1,
                    dev(d),
                )
                copy.start()
                copies.append(copy)
        return copies

    base3 = base2 + 4 * REDUCE

    def send_back(s, thirds):
        pieces = []
        for h in range(2):
            for q in range(2):
                for copy in thirds[q][h * 3 : h * 3 + 3]:
                    copy.wait()
                at = x if h == 0 else z
                total = quad[s, h, q, at].astype(F32)
                for d in range(3):
                    total = total + got_quad[s, h, q, d].astype(F32)
                total = total.astype(BF16)
                pieces.extend((total[:, :512], total[:, 512:]))
        stack = jnp.concatenate(pieces, axis=0)
        value = jnp.dot(helpers[0], stack, preferred_element_type=F32).astype(BF16)
        reply[s] = value.reshape(8, 16, 512)
        copies = []
        for d in range(1, 8):
            copy = remote(
                reply.at[s, lax.rem(e + d, 8)],
                returned.at[s, e],
                sems,
                base3 + s * 7 + d - 1,
                dev_e(d),
            )
            copy.start()
            copies.append(copy)
        returned[s, e] = reply[s, e]
        return copies

    row, col = (lax.broadcasted_iota(jnp.int32, (128, 128), d) for d in range(2))
    moved = row // 32 * 32 + row // 4 % 2 * 16 + row // 8 % 4 * 4 + row % 4
    turn = jnp.where(col == moved, 1.0, 0.0).astype(BF16)
    swaps = []
    early[0].wait()
    early[1].wait()
    for s in range(2):
        left[s] = jnp.dot(turn, gated[s], preferred_element_type=F32).astype(BF16)
        for q in range(2):
            first[s, q] = product(s, other, q).astype(BF16)
        if s == 0:
            pl.semaphore_wait(barrier, len(friends))
        swaps.append(mixer_swap(s))
    early[2].wait()
    for s in range(2):
        for q in range(2):
            mine[s, q] = product(s, c, q)
    ones0 = mixer_first(0, swaps[0])
    ones1 = mixer_first(1, swaps[1])
    early[3].wait()
    early[4].wait()
    for s in range(2):
        pick, mix = tables(ids[s], route[s], c)
        picks.append(pick)
        mixes.append(mix)
    swap = swap_fields()
    row, col = (lax.broadcasted_iota(jnp.int32, (16, 32), d) for d in range(2))
    chosen = jnp.where(col == row // 4 * 16 + x * 4 + row % 4, 1.0, 0.0).astype(BF16)
    helpers.extend((swap, chosen))
    loads = []
    for i, (a, b) in enumerate(((gate_hbm, gate), (up_hbm, up), (down_hbm, down))):
        load = pltpu.make_async_copy(a.at[0], b, local.at[i])
        load.start()
        loads.append(load)
    twos0 = mixer_second(0, ones0)
    twos1 = mixer_second(1, ones1)
    last0 = mixer_third(0, twos0)
    rows_out(0, last0)
    last1 = mixer_third(1, twos1)
    first0 = first_gather(0)
    rows_out(1, last1)
    second0 = second_gather(0, first0)
    first1 = first_gather(1)
    third00 = third_gather(0, 0, second0)
    third01 = third_gather(0, 1, second0)
    second1 = second_gather(1, first1)
    for copy in third00 + third01:
        copy.wait()
    for load in loads[:2]:
        load.wait()
    compute(0, 0)
    compute(0, 1)
    third10 = third_gather(1, 0, second1)
    loads[2].wait()
    project(0, 0)
    hop00 = first_reduce(0, 0)
    third11 = third_gather(1, 1, second1)
    project(0, 1)
    hop01 = first_reduce(0, 1)
    full00 = second_reduce(0, 0, hop00)
    full01 = second_reduce(0, 1, hop01)
    for copy in third10 + third11:
        copy.wait()
    compute(1, 0)
    compute(1, 1)
    project(1, 0)
    hop10 = first_reduce(1, 0)
    quad00 = third_reduce(0, 0, full00)
    project(1, 1)
    hop11 = first_reduce(1, 1)
    quad01 = third_reduce(0, 1, full01)
    full10 = second_reduce(1, 0, hop10)
    full11 = second_reduce(1, 1, hop11)
    back0 = send_back(0, (quad00, quad01))
    quad10 = third_reduce(1, 0, full10)
    quad11 = third_reduce(1, 1, full11)
    back1 = send_back(1, (quad10, quad11))
    for s in range(2):
        for copy in (back0, back1)[s]:
            copy.wait()
        replies = returned[s].reshape(128, 512)
        high = mixes[s].astype(BF16)
        low = (mixes[s] - high.astype(F32)).astype(BF16)
        value = jnp.dot(high, replies, preferred_element_type=F32)
        value = value + jnp.dot(low, replies, preferred_element_type=F32)
        for k in range(8):
            cols = slice(k * 512, (k + 1) * 512)
            total = residual[s, :, cols] + value[k * 8 : (k + 1) * 8]
            out[s, :, cols] = jnp.where(c == 0, total[:4], total[4:])


def expert_layer(gated, weight, ids, route, layer_in, gate, up, down):
    vmem = pl.BlockSpec(memory_space=pltpu.VMEM)
    hbm = pl.BlockSpec(memory_space=pl.ANY)
    count = 14 + 2 * GATHER + 4 * REDUCE + 14
    return pl.pallas_call(
        expert_kernel,
        out_shape=jax.ShapeDtypeStruct((2, 4, 4096), F32),
        in_specs=[hbm] * 8,
        out_specs=vmem,
        scratch_shapes=[
            pltpu.VMEM((2, 128, 128), BF16),
            pltpu.VMEM((128, 4096), BF16),
            pltpu.VMEM((2, 2, 4), jnp.int32),
            pltpu.VMEM((2, 2, 4), F32),
            pltpu.VMEM((2, 32, 4096), BF16),
            pltpu.VMEM((2, 128, 128), BF16),
            pltpu.VMEM((2, 2, 128, 1024), BF16),
            pltpu.VMEM((2, 2, 128, 1024), F32),
            pltpu.VMEM((2, 2, 128, 1024), BF16),
            pltpu.VMEM((2, 2, 4, 4, 16, 512), BF16),
            pltpu.VMEM((2, 2, 3, 4, 16, 512), BF16),
            pltpu.VMEM((2, 2, 4, 16, 512), BF16),
            pltpu.VMEM((2, 2, 3, 16, 512), BF16),
            pltpu.VMEM((2, 2, 16, 512), F32),
            pltpu.VMEM((2, 2, 16, 512), F32),
            pltpu.VMEM((2, 8, 4096), F32),
            pltpu.VMEM((512, 4096), BF16),
            pltpu.VMEM((512, 4096), BF16),
            pltpu.VMEM((512, 4096), BF16),
            pltpu.VMEM((2, 8, 16, 512), BF16),
            pltpu.VMEM((2, 8, 16, 512), BF16),
            pltpu.VMEM((2, 2, 4, 4, 16, 2048), BF16),
            pltpu.VMEM((256, 512), BF16),
            pltpu.VMEM((2, 2, 2, 4, 4, 16, 1024), BF16),
            pltpu.VMEM((2, 2, 2, 2, 2, 16, 1024), BF16),
            pltpu.VMEM((2, 2, 2, 2, 4, 16, 1024), BF16),
            pltpu.VMEM((2, 2, 2, 4, 16, 1024), BF16),
            pltpu.VMEM((2, 2, 2, 3, 16, 1024), BF16),
            pltpu.VMEM((2, 8, 16, 512), BF16),
            pltpu.VMEM((2, 8, 16, 512), BF16),
            pltpu.SemaphoreType.DMA((9,)),
            pltpu.SemaphoreType.DMA((count,)),
            pltpu.SemaphoreType.DMA((count,)),
            pltpu.SemaphoreType.DMA((30,)),
            pltpu.SemaphoreType.DMA((30,)),
        ],
        compiler_params=pltpu.CompilerParams(
            collective_id=1, has_side_effects=True, vmem_limit_bytes=60 * MIB
        ),
        name="experts",
    )(gated, weight, ids, route, layer_in, gate, up, down)


def finish_kernel(value, out):
    out[...] = value[...].astype(BF16)


def finish(value):
    vmem = pl.BlockSpec(memory_space=pltpu.VMEM)
    return pl.pallas_call(
        finish_kernel,
        out_shape=jax.ShapeDtypeStruct(value.shape, BF16),
        in_specs=[vmem],
        out_specs=vmem,
        name="finish",
    )(value)


def shards(
    layer_in,
    conv_state,
    ssm_state,
    proj_inner,
    proj_gate,
    conv_weight,
    conv_bias,
    delta_down,
    state_proj,
    delta_up,
    delta_bias,
    decay_log,
    skip_gain,
    proj_out,
    expert_gate,
    expert_up,
    expert_down,
    expert_ids,
    route_weight,
):
    conv_final, activated, gate_branch, step_size, state_in = mixer_in(
        layer_in.reshape(256, 4096),
        proj_inner,
        proj_gate,
        jnp.transpose(conv_state, (1, 0, 2)),
        conv_weight,
        conv_bias[None],
        delta_down,
        state_proj.reshape(32, 128),
        delta_up,
        delta_bias[None],
    )
    gated, ssm_state, conv_final = recurrence(
        step_size.reshape(2, 128, 128),
        activated.reshape(2, 128, 128),
        gate_branch.reshape(2, 128, 128),
        state_in.reshape(2, 128, 64),
        decay_log,
        skip_gain[None],
        conv_final,
        ssm_state,
    )
    conv_final = jnp.transpose(conv_final, (1, 0, 2))
    layer_out = expert_layer(
        gated,
        proj_out,
        jnp.transpose(expert_ids, (0, 2, 1)),
        jnp.transpose(route_weight, (0, 2, 1)),
        layer_in,
        expert_gate,
        expert_up,
        expert_down,
    )
    return (finish(layer_out), conv_final, ssm_state)


def solution(mesh):
    channels = ("expert", "tensor")
    rows = ("dp", "expert", "tensor")
    placed = (
        P(None, "dp", None),
        P("dp", None, channels),
        P("dp", None, channels),
        P(None, channels),
        P(None, channels),
        P(None, channels),
        P(channels),
        P(channels, None),
        P(None, None, channels),
        P(None, channels),
        P(channels),
        P(None, channels),
        P(channels),
        P(channels, None),
        P("expert", ("dp", "tensor"), None),
        P("expert", ("dp", "tensor"), None),
        P("expert", ("dp", "tensor"), None),
        P(None, rows, None),
        P(None, rows, None),
    )
    return jax.shard_map(
        shards,
        mesh=mesh,
        in_specs=placed,
        out_specs=(P(None, rows, None), P("dp", None, channels), P("dp", None, channels)),
        check_vma=False,
    )
```
